32 devices in a mesh: mem: 4 (over y, x), brick: 8 (over z, core).
Axes of the slice: x: 2, y: 2, z: 4, core: 2. Of those that a mesh axis runs over, the one named last changes fastest.
Arguments:
- members: float32 [128, 131072], P('mem', 'brick'), may hold values from -6 to 6
- predicted: float32 [128, 40, 1024], P('brick', None, 'mem'), may hold values from -6 to 6
- perturbation: float32 [128, 40, 1024], P('brick', None, 'mem'), may hold values from -6 to 6
- observed: float32 [40, 1024], P(None, ('mem', 'brick')), may hold values from -6 to 6
- noise_std: float32 [40, 1024], P(None, ('mem', 'brick')), may hold values from 0.3 to 3
- taper_weights: bfloat16 [1024, 512], P(('mem', 'brick')), may hold values from 0.099609375 to 1
- foot_brick: int32 [1024, 1], P(('mem', 'brick')), may hold values from 0 to 7; in each aligned block of 32 rows (0 to 31, 32 to 63, ...) at most 8 rows name the same one
- foot_tiles: int32 [1024, 4], P(('mem', 'brick')), may hold values from 0 to 127
Outputs:
- updated: float32 [128, 131072], P('mem', 'brick')
The draws below stay inside these ranges and needn't reach their ends.
Inputs may be any that keep to these rules, and one draw needn't show every extreme that they name: `foot_brick`: among the 32 soundings of one owner (aligned blocks of rows) at most 8 have their footprint in one brick, and some brick receives exactly 8 from some owner in every draw. `foot_tiles`: tile numbers inside the sounding's brick.
All inputs are finite; a program needn't handle non-finite values.
Results may differ from the reference program's by a relative error of at most 0.012.
Values may be sent and summed in bfloat16 or wider, within the bound.
A program may use at most 64 MiB of HBM per device.

```python
import math
import jax
import jax.numpy as jnp
import numpy as np
from jax import lax

ENS = 128
GATES = 40
FT = 4
SND_DEV = 32
CELLS = 16384
CAP = 8
TILES = 128
SOUNDINGS = 1024
NCELLS = 131072
N_BRICK = 8


def set_ends(drawn, stream_key, low, top_value):
    longest = drawn.shape.index(max(drawn.shape))
    spots = []
    for shift in (0, 1):
        where = [jax.random.randint(jax.random.fold_in(stream_key, axis), (), 0, length) for axis, length in enumerate(drawn.shape)]
        where[longest] = (where[longest] + shift) % drawn.shape[longest]
        spots.append(tuple(where))
    return drawn.at[spots[0]].set(low).at[spots[1]].set(top_value)


def block_scale(key, extent, shards, least, largest):
    loudness = 1.0
    for dim, parts in shards:
        steps = jax.random.uniform(jax.random.fold_in(jax.random.fold_in(key, 6), dim), (parts,), jnp.float32, least / len(shards), largest / len(shards))
        loudness = loudness * jnp.repeat(jnp.exp(steps), extent[dim] // parts).reshape((-1,) + (1,) * (len(extent) - 1 - dim))
    return loudness


def routed_block(own_key, own, number, rows, count, top, limit, slope):
    sequence = jax.random.permutation(own_key, count)
    crowded, ordinary = load_shares(count, rows * top, limit, slope, True), load_shares(count, rows * top, limit, slope, False)
    places = jnp.arange(count)

    def named(sizes, turn):
        used = int((sizes > 0).sum())
        fixed = max(1, used // 4)
        passed = fixed + (places - fixed + turn * (used - fixed)) % max(1, count - fixed)
        return jnp.zeros((count,), jnp.int32).at[sequence[jnp.where(places < fixed, places, passed)]].set(jnp.asarray(sizes, jnp.int32))

    sizes = jnp.where(number % 4 == 0, named(crowded, number // 4), named(ordinary, number - number // 4 - 1))
    mixed = jax.random.permutation(jax.random.fold_in(own, 3), count)
    source_of, sink = mixed[0:count // 2 * 2:2], mixed[1:count // 2 * 2:2]
    room = jnp.minimum(sizes[source_of] - 1, limit - sizes[sink]) // 2
    room = jnp.where((source_of == sequence[0]) | (sink == sequence[0]) | (sizes[sink] == 0), 0, jnp.maximum(room, 0))
    passed = jax.random.randint(jax.random.fold_in(own, 4), (count // 2,), 0, 1 << 20) % (room + 1)
    sizes = sizes.at[source_of].add(-passed).at[sink].add(passed)
    labels = jnp.searchsorted(jnp.cumsum(sizes), jnp.arange(rows * top), side="right").astype(jnp.int32)
    table = labels.reshape(top, rows).T
    table = table[jax.random.permutation(jax.random.fold_in(own, 1), rows)]
    turn = jax.random.randint(jax.random.fold_in(own, 2), (rows, 1), 0, top)
    return jnp.take_along_axis(table, (jnp.arange(top)[None, :] + turn) % top, axis=1)


def load_shares(number_of, total, bound, lean, full):
    weights = [(1 << 20) // math.isqrt(standing ** lean) + 1 for standing in range(1, number_of + 1)]
    largest = bound if full else min(bound, max(-(-total // number_of), total * weights[0] // sum(weights)))
    least = 1 if total - largest >= number_of - 1 else 0
    holding, spare = [largest] + [least] * (number_of - 1), total - largest - least * (number_of - 1)
    while spare > 0:
        free = [i for i in range(1, number_of) if holding[i] < largest] or [i for i in range(1, number_of) if holding[i] < bound]
        mass, remaining = sum([weights[i] for i in free]), spare
        for i in free:
            more = min(bound - holding[i], max(1, remaining * weights[i] // mass), spare)
            holding[i] = holding[i] + more
            spare = spare - more
    return np.array(holding)


def noise(own_key, shape, spread, limit, cuts=(), kind=jnp.bfloat16):
    factor_of = block_scale(own_key, shape, cuts, -0.22, 0.18) if cuts else 1.0
    result = jax.random.normal(own_key, shape, jnp.float32) * spread * factor_of
    return jnp.minimum(jnp.maximum(result, -limit), limit).astype(kind)


def setup_inputs(seed: int = 0) -> dict:
    splits = jax.random.split(jax.random.key(seed), 9)
    members = noise(splits[0], (ENS, NCELLS), 1.0, 6.0, ((0, 4), (1, 8)), jnp.float32)
    predicted = noise(splits[1], (ENS, GATES, SOUNDINGS), 1.0, 6.0, ((0, 8), (2, 4)), jnp.float32)
    perturbation = noise(splits[2], (ENS, GATES, SOUNDINGS), 1.0, 6.0, ((0, 8), (2, 4)), jnp.float32)
    observed = noise(splits[3], (GATES, SOUNDINGS), 1.0, 6.0, ((1, 32),), jnp.float32)
    noise_std = jnp.clip(jnp.exp(math.log(3.0) - 2.3025851 * jax.random.uniform(splits[4], (GATES, SOUNDINGS), jnp.float32) ** block_scale(splits[4], (GATES, SOUNDINGS), ((1, 32),), -0.2, 0.2)), 0.3, 3.0)
    taper_weights = jnp.clip(0.099609375 + 0.9003906 * jax.random.uniform(splits[5], (SOUNDINGS, FT * 128), jnp.float32) ** block_scale(splits[5], (SOUNDINGS, FT * 128), ((0, 32),), -0.2, 0.2), 0.099609375, 1.0).astype(jnp.bfloat16)
    foot_brick_keys = jax.random.split(jax.random.fold_in(splits[6], 1), SOUNDINGS // SND_DEV)
    foot_brick_turns = jax.random.permutation(jax.random.fold_in(splits[6], 3), SOUNDINGS // SND_DEV)
    foot_brick = jax.vmap(lambda own, number: routed_block(jax.random.fold_in(splits[6], 2), own, number, SND_DEV, N_BRICK, 1, CAP, 2))(foot_brick_keys, foot_brick_turns).reshape((SOUNDINGS, 1))
    foot_tiles = set_ends(jax.random.randint(splits[7], (SOUNDINGS, FT), 0, CELLS // 128), jax.random.fold_in(splits[7], 1), 0, (CELLS // 128) - 1).astype(jnp.int32)
    return {"members": members, "predicted": predicted, "perturbation": perturbation, "observed": observed, "noise_std": noise_std, "taper_weights": taper_weights, "foot_brick": foot_brick, "foot_tiles": foot_tiles}


def owner_factors(predicted, perturbation, observed, noise_std):
    ensemble = predicted.shape[0]
    gate_count = predicted.shape[1]
    gate_mean = jnp.mean(predicted, axis=0)
    anomaly = predicted - gate_mean[None]
    covariance = jnp.einsum('jgs,jhs->sgh', anomaly, anomaly, precision=lax.Precision.HIGHEST) / (ensemble - 1.0)
    variance = jnp.transpose(noise_std * noise_std)
    covariance = covariance + variance[:, :, None] * jnp.eye(gate_count, dtype=jnp.float32)[None]
    misfit = observed[None] + noise_std[None] * perturbation - predicted
    lower = jnp.linalg.cholesky(covariance)
    right_side = jnp.transpose(misfit, (2, 1, 0))
    halfway = jax.scipy.linalg.solve_triangular(lower, right_side, lower=True)
    solved = jax.scipy.linalg.solve_triangular(lower, halfway, lower=True, trans=1) / (ensemble - 1.0)
    gain_rows = jnp.transpose(solved, (0, 2, 1)).astype(jnp.bfloat16)
    anomaly_rows = jnp.transpose(anomaly, (2, 0, 1)).astype(jnp.bfloat16)
    return (anomaly_rows, gain_rows)

def reference(members, predicted, perturbation, observed, noise_std, taper_weights, foot_brick, foot_tiles):
    anomaly_rows, gain_rows = owner_factors(predicted, perturbation, observed, noise_std)
    tile_count = members.shape[1] // 128
    model_tiles = members.astype(jnp.bfloat16).reshape(ENS, tile_count, 128)
    global_tiles = (foot_brick[:, 0:1] * TILES + foot_tiles).astype(jnp.int32)
    block_size = math.gcd(SOUNDINGS, 256)
    step_count = SOUNDINGS // block_size

    def one_block(accumulated, pieces):
        anomaly_block, gain_block, taper_block, tile_block = pieces
        flat_tiles = tile_block.reshape(-1)
        gathered = model_tiles[:, flat_tiles].reshape(ENS, block_size, FT * 128)
        gate_field = jnp.einsum('bjg,jbp->bgp', anomaly_block.astype(jnp.float32), gathered.astype(jnp.float32), precision=lax.Precision.HIGHEST)
        gate_field = gate_field.astype(jnp.bfloat16)
        contribution = jnp.einsum('bjg,bgp->jbp', gain_block.astype(jnp.float32), gate_field.astype(jnp.float32), precision=lax.Precision.HIGHEST)
        contribution = contribution * taper_block.astype(jnp.float32)[None]
        accumulated = accumulated.at[:, flat_tiles].add(contribution.reshape(ENS, block_size * FT, 128))
        return (accumulated, None)
    start = jnp.zeros((ENS, tile_count, 128), jnp.float32)
    stacked = (anomaly_rows.reshape(step_count, block_size, ENS, GATES), gain_rows.reshape(step_count, block_size, ENS, GATES), taper_weights.reshape(step_count, block_size, FT * 128), global_tiles.reshape(step_count, block_size, FT))
    accumulated, _ = lax.scan(one_block, start, stacked)
    return members + accumulated.reshape(members.shape)
```

```python
import jax
import jax.numpy as jnp
from jax import lax
from jax.experimental import pallas as pl
from jax.experimental.pallas import tpu as pltpu
from jax.sharding import PartitionSpec as P

GROUP = 4
HIGH = lax.Precision.HIGHEST


def factor_kernel(
    slot_ref, data_ref, obs_ref, std_ref, taper_ref, out_ref, anom, misf, cov, work, inv
):
    peers, soundings, part, lanes = data_ref.shape
    ensemble = peers * part
    gates = obs_ref.shape[1]
    mem_count = out_ref.shape[0]
    bricks = out_ref.shape[1]
    cap = out_ref.shape[2] - 1
    block = out_ref.shape[3]

    for m in range(mem_count):
        for b in range(bricks):
            out_ref[m, b, cap] = taper_ref[b]

    row = lax.broadcasted_iota(jnp.int32, (gates, gates), 0)
    column = lax.broadcasted_iota(jnp.int32, (gates, gates), 1)

    def prepare(s, carry):
        rows = data_ref[:, s].astype(jnp.float32).reshape(ensemble, lanes)
        turned = rows.T
        pred = turned[:gates]
        pert = turned[gates : 2 * gates]
        std = std_ref[s]
        anomaly = pred - jnp.sum(pred, axis=1, keepdims=True) / ensemble
        misf[s] = obs_ref[s] + std * pert - pred
        anom[s] = anomaly
        total = lax.dot_general(
            anomaly,
            anomaly,
            (((1,), (1,)), ((), ())),
            precision=HIGH,
            preferred_element_type=jnp.float32,
        ) / (ensemble - 1.0)
        cov[s] = total + jnp.where(row == column, std * std, 0.0)
        return carry

    lax.fori_loop(0, soundings, prepare, 0, unroll=2)

    for i in range(gates):
        work[i] = cov[:, i, :].T

    place = lax.broadcasted_iota(jnp.int32, (gates, soundings), 0)

    def sweep(k, carry):
        scale = 1.0 / work[k, pl.ds(k, 1), :]
        pivot = work[k]
        scaled = jnp.where(place == k, scale, pivot * scale)
        held = jnp.where(place == k, 0.0, 1.0)
        for i in range(gates):
            coef = work[i, pl.ds(k, 1), :]
            work[i] = work[i] * held - coef * scaled
        work[k] = scaled
        return carry

    lax.fori_loop(0, gates, sweep, 0)

    for i in range(gates):
        inv[:, i, :] = work[i].T

    def finish(s, carry):
        gain = lax.dot_general(
            inv[s],
            misf[s],
            (((1,), (0,)), ((), ())),
            precision=HIGH,
            preferred_element_type=jnp.float32,
        ) / (ensemble - 1.0)
        weight = lax.dot_general(
            gain.T.astype(jnp.bfloat16),
            anom[s].astype(jnp.bfloat16),
            (((1,), (0,)), ((), ())),
            preferred_element_type=jnp.float32,
        ).astype(jnp.bfloat16)
        brick = slot_ref[0, s]
        rank = slot_ref[1, s]
        for m in range(mem_count):
            out_ref[m, brick, rank] = weight[m * block : (m + 1) * block]
        return carry

    lax.fori_loop(0, soundings, finish, 0, unroll=2)


def update_kernel(count_ref, owner_ref, rank_ref, tile_ref, recv_ref, model_ref, members_ref, out_ref):
    cap = recv_ref.shape[1] - 1
    foot = tile_ref.shape[0]
    total = count_ref[0]
    out_ref[...] = members_ref[...]

    def turn(step, carry):
        results = []
        for u in range(GROUP):
            at = step * GROUP + u
            owner = owner_ref[at]
            rank = rank_ref[at]
            weight = recv_ref[owner, rank]
            taper = recv_ref[owner, cap, : cap * foot].astype(jnp.float32).reshape(cap, foot, 128)
            mine = lax.broadcasted_iota(jnp.int32, (cap, foot, 128), 0) == rank
            taper = jnp.sum(jnp.where(mine, taper, 0.0), axis=0)
            used = at < total
            for c in range(foot):
                start = pl.multiple_of(tile_ref[c, at] * 128, 128)
                part = jnp.dot(
                    weight, model_ref[:, pl.ds(start, 128)], preferred_element_type=jnp.float32
                )
                results.append((start, jnp.where(used, part * taper[c : c + 1], 0.0)))
        for start, part in results:
            out_ref[:, pl.ds(start, 128)] += part
        return carry

    lax.fori_loop(0, (total + GROUP - 1) // GROUP, turn, 0)


def body(
    members, predicted, perturbation, observed, noise_std, taper_weights, foot_brick, foot_tiles
):
    mem_count = lax.axis_size("mem")
    brick_count = lax.axis_size("brick")
    part, gates, wide = predicted.shape
    ensemble = part * brick_count
    local = wide // brick_count
    block = ensemble // mem_count
    foot = foot_tiles.shape[1]
    foot_length = taper_weights.shape[1]
    devices = mem_count * brick_count
    cap = max(2, 2 * local // brick_count)
    rows = cap * foot
    slots = devices * cap
    vmem = pltpu.CompilerParams(vmem_limit_bytes=48 * 1024 * 1024)
    in_vmem = pl.BlockSpec(memory_space=pltpu.VMEM)
    in_smem = pl.BlockSpec(memory_space=pltpu.SMEM)

    model_all = lax.all_gather(members.astype(jnp.bfloat16), "mem", axis=0, tiled=True)

    pair = jnp.concatenate([predicted, perturbation], axis=1).astype(jnp.bfloat16)
    pair = jnp.transpose(pair, (2, 0, 1))
    pair = jnp.pad(pair, ((0, 0), (0, 0), (0, 128 - 2 * gates)))
    pair = pair.reshape(brick_count, local, part, 128)
    data = lax.all_to_all(pair, "brick", split_axis=0, concat_axis=0, tiled=True)

    feet = jnp.concatenate([foot_brick, foot_tiles], axis=1)
    feet = lax.all_gather(feet, ("mem", "brick"), axis=0, tiled=True)

    destination = foot_brick[:, 0]
    order = jnp.arange(local)
    before = order[None, :] < order[:, None]
    rank = jnp.sum(
        ((destination[:, None] == destination[None, :]) & before).astype(jnp.int32), axis=1
    )
    slot_table = jnp.stack([destination, rank])
    selector = (
        (destination * cap + rank)[None, :] == jnp.arange(brick_count * cap, dtype=jnp.int32)[:, None]
    ).astype(jnp.bfloat16)
    taper_slots = jnp.dot(selector, taper_weights, preferred_element_type=jnp.float32)
    taper_slots = taper_slots.astype(jnp.bfloat16).reshape(brick_count, rows, 128)
    if rows < block:
        taper_slots = jnp.pad(taper_slots, ((0, 0), (0, block - rows), (0, 0)))

    send = pl.pallas_call(
        factor_kernel,
        out_shape=jax.ShapeDtypeStruct(
            (mem_count, brick_count, cap + 1, block, 128), jnp.bfloat16
        ),
        in_specs=[in_smem] + [in_vmem] * 4,
        out_specs=in_vmem,
        scratch_shapes=[
            pltpu.VMEM((local, gates, ensemble), jnp.float32),
            pltpu.VMEM((local, gates, ensemble), jnp.float32),
            pltpu.VMEM((local, gates, gates), jnp.float32),
            pltpu.VMEM((gates, gates, local), jnp.float32),
            pltpu.VMEM((local, gates, gates), jnp.float32),
        ],
        compiler_params=vmem,
        cost_estimate=pl.CostEstimate(flops=400_000_000, bytes_accessed=5_000_000, transcendentals=0),
    )(
        slot_table,
        data,
        jnp.transpose(observed)[:, :, None],
        jnp.transpose(noise_std)[:, :, None],
        taper_slots,
    )
    recv = lax.all_to_all(
        send.reshape(devices, (cap + 1) * block, 128),
        ("mem", "brick"),
        split_axis=0,
        concat_axis=0,
        tiled=True,
    ).reshape(devices, cap + 1, block, 128)

    here = lax.axis_index("brick")
    feet = feet.reshape(devices, local, 1 + foot)
    bricks = feet[:, :, 0]
    mine = bricks == here
    ranks = jnp.sum((mine[:, None, :] & before[None]).astype(jnp.int32), axis=2)
    counts = jnp.sum(mine.astype(jnp.int32), axis=1)
    owners = jnp.arange(devices)
    starts = jnp.sum(
        jnp.where(owners[None, :] < owners[:, None], counts[None, :], 0), axis=1
    )
    position = jnp.where(mine, starts[:, None] + ranks, -1).reshape(-1)
    hot = position[None, :] == jnp.arange(slots)[:, None]
    owner_of = jnp.broadcast_to(owners[:, None], mine.shape).reshape(-1)

    def listed(values):
        return jnp.sum(jnp.where(hot, values[None, :], 0), axis=1)

    owner_list = listed(owner_of)
    rank_list = listed(ranks.reshape(-1))
    tile_list = jnp.stack([listed(feet[:, :, 1 + c].reshape(-1)) for c in range(foot)])
    count = jnp.sum(counts).reshape(1)

    return pl.pallas_call(
        update_kernel,
        out_shape=jax.ShapeDtypeStruct(members.shape, members.dtype),
        in_specs=[in_smem] * 4 + [in_vmem] * 3,
        out_specs=in_vmem,
        compiler_params=vmem,
        cost_estimate=pl.CostEstimate(flops=600_000_000, bytes_accessed=10_000_000, transcendentals=0),
    )(count, owner_list, rank_list, tile_list, recv, model_all, members)


def solution(mesh):
    in_specs = (
        P("mem", "brick"),
        P("brick", None, "mem"),
        P("brick", None, "mem"),
        P(None, ("mem", "brick")),
        P(None, ("mem", "brick")),
        P(("mem", "brick"), None),
        P(("mem", "brick"), None),
        P(("mem", "brick"), None),
    )
    out_specs = P("mem", "brick")
    return jax.shard_map(body, mesh=mesh, in_specs=in_specs, out_specs=out_specs, check_vma=False)
```

```python
import jax
import jax.numpy as jnp
from jax import lax
from jax.experimental import pallas as pl
from jax.experimental.pallas import tpu as pltpu
from jax.sharding import PartitionSpec as P

GROUP = 4
HIGH = lax.Precision.HIGHEST


def factor_kernel(data_ref, obs_ref, std_ref, out_ref, anom, misf, cov, work, inv):
    peers, soundings, part, lanes = data_ref.shape
    ensemble = peers * part
    gates = obs_ref.shape[1]

    row = lax.broadcasted_iota(jnp.int32, (gates, gates), 0)
    column = lax.broadcasted_iota(jnp.int32, (gates, gates), 1)

    def prepare(s, carry):
        rows = data_ref[:, s].astype(jnp.float32).reshape(ensemble, lanes)
        turned = rows.T
        pred = turned[:gates]
        pert = turned[gates : 2 * gates]
        std = std_ref[s]
        anomaly = pred - jnp.sum(pred, axis=1, keepdims=True) / ensemble
        misf[s] = obs_ref[s] + std * pert - pred
        anom[s] = anomaly
        total = lax.dot_general(
            anomaly,
            anomaly,
            (((1,), (1,)), ((), ())),
            precision=HIGH,
            preferred_element_type=jnp.float32,
        ) / (ensemble - 1.0)
        cov[s] = total + jnp.where(row == column, std * std, 0.0)
        return carry

    lax.fori_loop(0, soundings, prepare, 0, unroll=2)

    for i in range(gates):
        work[i] = cov[:, i, :].T

    place = lax.broadcasted_iota(jnp.int32, (gates, soundings), 0)

    def sweep(k, carry):
        scale = 1.0 / work[k, pl.ds(k, 1), :]
        pivot = work[k]
        scaled = jnp.where(place == k, scale, pivot * scale)
        held = jnp.where(place == k, 0.0, 1.0)
        for i in range(gates):
            coef = work[i, pl.ds(k, 1), :]
            work[i] = work[i] * held - coef * scaled
        work[k] = scaled
        return carry

    lax.fori_loop(0, gates, sweep, 0)

    for i in range(gates):
        inv[:, i, :] = work[i].T

    def finish(s, carry):
        gain = lax.dot_general(
            inv[s],
            misf[s],
            (((1,), (0,)), ((), ())),
            precision=HIGH,
            preferred_element_type=jnp.float32,
        ) / (ensemble - 1.0)
        out_ref[s] = jnp.concatenate([gain, anom[s]], axis=0).astype(jnp.bfloat16)
        return carry

    lax.fori_loop(0, soundings, finish, 0, unroll=2)


def exchange_kernel(
    index_ref, fact_ref, taper_ref, out_ref, stage, landed, spread, z_send, z_recv, m_send, m_recv
):
    mem_count, bricks, out_rows, _ = out_ref.shape
    pair_rows = fact_ref.shape[1]
    gates = pair_rows // 2
    block = taper_ref.shape[1]
    cap = (out_rows - block) // block
    at_m = lax.axis_index("mem")
    at_b = lax.axis_index("brick")

    barrier = pltpu.get_barrier_semaphore()
    for d in range(1, bricks):
        pl.semaphore_signal(
            barrier,
            inc=1,
            device_id=(at_m, lax.rem(at_b + d, bricks)),
            device_id_type=pl.DeviceIdType.MESH,
        )
    for e in range(1, mem_count):
        pl.semaphore_signal(
            barrier,
            inc=1,
            device_id=(lax.rem(at_m + e, mem_count), at_b),
            device_id_type=pl.DeviceIdType.MESH,
        )
    pl.semaphore_wait(barrier, bricks + mem_count - 2)

    def to_brick(d):
        there = lax.rem(at_b + d, bricks)
        return pltpu.make_async_remote_copy(
            src_ref=stage.at[there],
            dst_ref=landed.at[at_b],
            send_sem=z_send.at[d],
            recv_sem=z_recv.at[d],
            device_id=(at_m, there),
            device_id_type=pl.DeviceIdType.MESH,
        )

    def to_member(d, e):
        source = lax.rem(at_b - d + bricks, bricks)
        there = lax.rem(at_m + e, mem_count)
        return pltpu.make_async_remote_copy(
            src_ref=spread.at[source, there],
            dst_ref=out_ref.at[at_m, source],
            send_sem=m_send.at[d * mem_count + e],
            recv_sem=m_recv.at[d * mem_count + e],
            device_id=(there, at_b),
            device_id_type=pl.DeviceIdType.MESH,
        )

    def pack(ref, place, there):
        for r in range(cap):
            ref[place, pl.ds(r * pair_rows, pair_rows), :] = fact_ref[index_ref[there * cap + r]]
        ref[place, pl.ds(cap * pair_rows, block), :] = taper_ref[there]

    def post(d, carry):
        there = lax.rem(at_b + d, bricks)
        pack(stage, there, there)
        to_brick(d).start()
        return carry

    lax.fori_loop(1, bricks, post, 0)
    pack(landed, at_b, at_b)

    def weigh(d):
        source = lax.rem(at_b - d + bricks, bricks)
        for r in range(cap):
            pair = landed[source, pl.ds(r * pair_rows, pair_rows), :].astype(jnp.float32)
            weight = jnp.dot(
                pair[:gates].T.astype(jnp.bfloat16),
                pair[gates:].astype(jnp.bfloat16),
                preferred_element_type=jnp.float32,
            ).astype(jnp.bfloat16)
            for m in range(mem_count):
                spread[source, m, pl.ds(r * block, block), :] = weight[m * block : (m + 1) * block]
        tapers = landed[source, pl.ds(cap * pair_rows, block), :]
        for m in range(mem_count):
            spread[source, m, pl.ds(cap * block, block), :] = tapers
        for e in range(1, mem_count):
            to_member(d, e).start()
        out_ref[at_m, source] = spread[source, at_m]

    weigh(0)

    def take(d, carry):
        to_brick(d).wait_recv()
        weigh(d)
        return carry

    lax.fori_loop(1, bricks, take, 0)

    def sent(d, carry):
        to_brick(d).wait_send()
        return carry

    lax.fori_loop(1, bricks, sent, 0)

    def settle(d, carry):
        for e in range(1, mem_count):
            to_member(d, e).wait()
        return carry

    lax.fori_loop(0, bricks, settle, 0)


def update_kernel(count_ref, owner_ref, rank_ref, tile_ref, recv_ref, model_ref, members_ref, out_ref):
    cap = recv_ref.shape[1] - 1
    foot = tile_ref.shape[0]
    total = count_ref[0]
    out_ref[...] = members_ref[...]

    def turn(step, carry):
        results = []
        for u in range(GROUP):
            at = step * GROUP + u
            owner = owner_ref[at]
            rank = rank_ref[at]
            weight = recv_ref[owner, rank]
            taper = recv_ref[owner, cap, : cap * foot].astype(jnp.float32).reshape(cap, foot, 128)
            mine = lax.broadcasted_iota(jnp.int32, (cap, foot, 128), 0) == rank
            taper = jnp.sum(jnp.where(mine, taper, 0.0), axis=0)
            used = at < total
            for c in range(foot):
                start = pl.multiple_of(tile_ref[c, at] * 128, 128)
                part = jnp.dot(
                    weight, model_ref[:, pl.ds(start, 128)], preferred_element_type=jnp.float32
                )
                results.append((start, jnp.where(used, part * taper[c : c + 1], 0.0)))
        for start, part in results:
            out_ref[:, pl.ds(start, 128)] += part
        return carry

    lax.fori_loop(0, (total + GROUP - 1) // GROUP, turn, 0)


def body(
    members, predicted, perturbation, observed, noise_std, taper_weights, foot_brick, foot_tiles
):
    mem_count = lax.axis_size("mem")
    brick_count = lax.axis_size("brick")
    part, gates, wide = predicted.shape
    ensemble = part * brick_count
    local = wide // brick_count
    block = ensemble // mem_count
    foot = foot_tiles.shape[1]
    foot_length = taper_weights.shape[1]
    devices = mem_count * brick_count
    cap = max(2, 2 * local // brick_count)
    rows = cap * foot
    slots = devices * cap
    vmem = pltpu.CompilerParams(vmem_limit_bytes=48 * 1024 * 1024)
    in_vmem = pl.BlockSpec(memory_space=pltpu.VMEM)
    in_smem = pl.BlockSpec(memory_space=pltpu.SMEM)

    model_all = lax.all_gather(members.astype(jnp.bfloat16), "mem", axis=0, tiled=True)

    pair = jnp.concatenate([predicted, perturbation], axis=1).astype(jnp.bfloat16)
    pair = jnp.transpose(pair, (2, 0, 1))
    pair = jnp.pad(pair, ((0, 0), (0, 0), (0, 128 - 2 * gates)))
    pair = pair.reshape(brick_count, local, part, 128)
    data = lax.all_to_all(pair, "brick", split_axis=0, concat_axis=0, tiled=True)

    feet = jnp.concatenate([foot_brick, foot_tiles], axis=1)
    feet = lax.all_gather(feet, ("mem", "brick"), axis=0, tiled=True)

    destination = foot_brick[:, 0]
    order = jnp.arange(local)
    before = order[None, :] < order[:, None]
    rank = jnp.sum(
        ((destination[:, None] == destination[None, :]) & before).astype(jnp.int32), axis=1
    )
    selector = (
        (destination * cap + rank)[None, :] == jnp.arange(brick_count * cap, dtype=jnp.int32)[:, None]
    ).astype(jnp.bfloat16)
    taper_slots = jnp.dot(selector, taper_weights, preferred_element_type=jnp.float32)
    taper_slots = taper_slots.astype(jnp.bfloat16).reshape(brick_count, rows, 128)
    if rows < block:
        taper_slots = jnp.pad(taper_slots, ((0, 0), (0, block - rows), (0, 0)))

    slot_of = destination * cap + rank
    index = jnp.sum(
        jnp.where(
            slot_of[None, :] == jnp.arange(brick_count * cap)[:, None], order[None, :], 0
        ),
        axis=1,
    )

    fact = pl.pallas_call(
        factor_kernel,
        out_shape=jax.ShapeDtypeStruct((local, 2 * gates, ensemble), jnp.bfloat16),
        in_specs=[in_vmem] * 3,
        out_specs=in_vmem,
        scratch_shapes=[
            pltpu.VMEM((local, gates, ensemble), jnp.float32),
            pltpu.VMEM((local, gates, ensemble), jnp.float32),
            pltpu.VMEM((local, gates, gates), jnp.float32),
            pltpu.VMEM((gates, gates, local), jnp.float32),
            pltpu.VMEM((local, gates, gates), jnp.float32),
        ],
        compiler_params=vmem,
        cost_estimate=pl.CostEstimate(flops=400_000_000, bytes_accessed=5_000_000, transcendentals=0),
    )(data, jnp.transpose(observed)[:, :, None], jnp.transpose(noise_std)[:, :, None])

    packed_rows = cap * 2 * gates + block
    out_rows = (cap + 1) * block
    recv = pl.pallas_call(
        exchange_kernel,
        out_shape=jax.ShapeDtypeStruct((mem_count, brick_count, out_rows, 128), jnp.bfloat16),
        in_specs=[in_smem] + [in_vmem] * 2,
        out_specs=in_vmem,
        scratch_shapes=[
            pltpu.VMEM((brick_count, packed_rows, 128), jnp.bfloat16),
            pltpu.VMEM((brick_count, packed_rows, 128), jnp.bfloat16),
            pltpu.VMEM((brick_count, mem_count, out_rows, 128), jnp.bfloat16),
            pltpu.SemaphoreType.DMA((brick_count,)),
            pltpu.SemaphoreType.DMA((brick_count,)),
            pltpu.SemaphoreType.DMA((brick_count * mem_count,)),
            pltpu.SemaphoreType.DMA((brick_count * mem_count,)),
        ],
        compiler_params=pltpu.CompilerParams(
            vmem_limit_bytes=48 * 1024 * 1024, collective_id=0, has_side_effects=True
        ),
        cost_estimate=pl.CostEstimate(flops=100_000_000, bytes_accessed=8_000_000, transcendentals=0),
    )(index, fact, taper_slots).reshape(devices, cap + 1, block, 128)

    here = lax.axis_index("brick")
    feet = feet.reshape(devices, local, 1 + foot)
    bricks = feet[:, :, 0]
    mine = bricks == here
    ranks = jnp.sum((mine[:, None, :] & before[None]).astype(jnp.int32), axis=2)
    counts = jnp.sum(mine.astype(jnp.int32), axis=1)
    owners = jnp.arange(devices)
    starts = jnp.sum(
        jnp.where(owners[None, :] < owners[:, None], counts[None, :], 0), axis=1
    )
    position = jnp.where(mine, starts[:, None] + ranks, -1).reshape(-1)
    hot = position[None, :] == jnp.arange(slots)[:, None]
    owner_of = jnp.broadcast_to(owners[:, None], mine.shape).reshape(-1)

    def listed(values):
        return jnp.sum(jnp.where(hot, values[None, :], 0), axis=1)

    owner_list = listed(owner_of)
    rank_list = listed(ranks.reshape(-1))
    tile_list = jnp.stack([listed(feet[:, :, 1 + c].reshape(-1)) for c in range(foot)])
    count = jnp.sum(counts).reshape(1)

    return pl.pallas_call(
        update_kernel,
        out_shape=jax.ShapeDtypeStruct(members.shape, members.dtype),
        in_specs=[in_smem] * 4 + [in_vmem] * 3,
        out_specs=in_vmem,
        compiler_params=vmem,
        cost_estimate=pl.CostEstimate(flops=600_000_000, bytes_accessed=10_000_000, transcendentals=0),
    )(count, owner_list, rank_list, tile_list, recv, model_all, members)


def solution(mesh):
    in_specs = (
        P("mem", "brick"),
        P("brick", None, "mem"),
        P("brick", None, "mem"),
        P(None, ("mem", "brick")),
        P(None, ("mem", "brick")),
        P(("mem", "brick"), None),
        P(("mem", "brick"), None),
        P(("mem", "brick"), None),
    )
    out_specs = P("mem", "brick")
    return jax.shard_map(body, mesh=mesh, in_specs=in_specs, out_specs=out_specs, check_vma=False)
```

```python
import jax
import jax.numpy as jnp
from jax import lax
from jax.experimental import pallas as pl
from jax.experimental.pallas import tpu as pltpu
from jax.sharding import PartitionSpec as P

GROUP = 4
HIGH = lax.Precision.HIGHEST


def factor_kernel(data_ref, obs_ref, std_ref, out_ref, anom, misf, cov, work, inv):
    peers, soundings, part, lanes = data_ref.shape
    ensemble = peers * part
    gates = obs_ref.shape[1]

    row = lax.broadcasted_iota(jnp.int32, (gates, gates), 0)
    column = lax.broadcasted_iota(jnp.int32, (gates, gates), 1)

    def prepare(s, carry):
        rows = data_ref[:, s].astype(jnp.float32).reshape(ensemble, lanes)
        turned = rows.T
        pred = turned[:gates]
        pert = turned[gates : 2 * gates]
        std = std_ref[s]
        anomaly = pred - jnp.sum(pred, axis=1, keepdims=True) / ensemble
        misf[s] = obs_ref[s] + std * pert - pred
        anom[s] = anomaly
        total = lax.dot_general(
            anomaly,
            anomaly,
            (((1,), (1,)), ((), ())),
            precision=HIGH,
            preferred_element_type=jnp.float32,
        ) / (ensemble - 1.0)
        cov[s] = total + jnp.where(row == column, std * std, 0.0)
        return carry

    lax.fori_loop(0, soundings, prepare, 0, unroll=2)

    for i in range(gates):
        work[i] = cov[:, i, :].T

    place = lax.broadcasted_iota(jnp.int32, (gates, soundings), 0)

    def sweep(k, carry):
        scale = 1.0 / work[k, pl.ds(k, 1), :]
        pivot = work[k]
        scaled = jnp.where(place == k, scale, pivot * scale)
        held = jnp.where(place == k, 0.0, 1.0)
        for i in range(gates):
            coef = work[i, pl.ds(k, 1), :]
            work[i] = work[i] * held - coef * scaled
        work[k] = scaled
        return carry

    lax.fori_loop(0, gates, sweep, 0)

    for i in range(gates):
        inv[:, i, :] = work[i].T

    def finish(s, carry):
        gain = lax.dot_general(
            inv[s],
            misf[s],
            (((1,), (0,)), ((), ())),
            precision=HIGH,
            preferred_element_type=jnp.float32,
        ) / (ensemble - 1.0)
        out_ref[s] = jnp.concatenate([gain, anom[s]], axis=0).astype(jnp.bfloat16)
        return carry

    lax.fori_loop(0, soundings, finish, 0, unroll=2)


def exchange_kernel(
    index_ref, fact_ref, taper_ref, out_ref, stage, landed, spread, z_send, z_recv, m_send, m_recv
):
    mem_count, bricks, out_rows, _ = out_ref.shape
    pair_rows = fact_ref.shape[1]
    gates = pair_rows // 2
    tail = taper_ref.shape[1]
    cap = index_ref.shape[0] // bricks
    block = (out_rows - tail) // cap
    at_m = lax.axis_index("mem")
    at_b = lax.axis_index("brick")

    barrier = pltpu.get_barrier_semaphore()
    for d in range(1, bricks):
        pl.semaphore_signal(
            barrier,
            inc=1,
            device_id=(at_m, lax.rem(at_b + d, bricks)),
            device_id_type=pl.DeviceIdType.MESH,
        )
    for e in range(1, mem_count):
        pl.semaphore_signal(
            barrier,
            inc=1,
            device_id=(lax.rem(at_m + e, mem_count), at_b),
            device_id_type=pl.DeviceIdType.MESH,
        )
    pl.semaphore_wait(barrier, bricks + mem_count - 2)

    def to_brick(d):
        there = lax.rem(at_b + d, bricks)
        return pltpu.make_async_remote_copy(
            src_ref=stage.at[there],
            dst_ref=landed.at[at_b],
            send_sem=z_send.at[d],
            recv_sem=z_recv.at[d],
            device_id=(at_m, there),
            device_id_type=pl.DeviceIdType.MESH,
        )

    def to_member(d, e):
        source = lax.rem(at_b - d + bricks, bricks)
        there = lax.rem(at_m + e, mem_count)
        return pltpu.make_async_remote_copy(
            src_ref=spread.at[source, there],
            dst_ref=out_ref.at[at_m, source],
            send_sem=m_send.at[d * mem_count + e],
            recv_sem=m_recv.at[d * mem_count + e],
            device_id=(there, at_b),
            device_id_type=pl.DeviceIdType.MESH,
        )

    def pack(ref, place, there):
        for r in range(cap):
            ref[place, pl.ds(r * pair_rows, pair_rows), :] = fact_ref[index_ref[there * cap + r]]
        ref[place, pl.ds(cap * pair_rows, tail), :] = taper_ref[there]

    def post(d, carry):
        there = lax.rem(at_b + d, bricks)
        pack(stage, there, there)
        to_brick(d).start()
        return carry

    lax.fori_loop(1, bricks, post, 0)
    pack(landed, at_b, at_b)

    def weigh(d):
        source = lax.rem(at_b - d + bricks, bricks)
        for r in range(cap):
            pair = landed[source, pl.ds(r * pair_rows, pair_rows), :].astype(jnp.float32)
            weight = jnp.dot(
                pair[:gates].T.astype(jnp.bfloat16),
                pair[gates:].astype(jnp.bfloat16),
                preferred_element_type=jnp.float32,
            ).astype(jnp.bfloat16)
            for m in range(mem_count):
                spread[source, m, pl.ds(r * block, block), :] = weight[m * block : (m + 1) * block]
        tapers = landed[source, pl.ds(cap * pair_rows, tail), :]
        for m in range(mem_count):
            spread[source, m, pl.ds(cap * block, tail), :] = tapers
        for e in range(1, mem_count):
            to_member(d, e).start()
        out_ref[at_m, source] = spread[source, at_m]

    weigh(0)

    def take(d, carry):
        to_brick(d).wait_recv()
        weigh(d)
        return carry

    lax.fori_loop(1, bricks, take, 0)

    def sent(d, carry):
        to_brick(d).wait_send()
        return carry

    lax.fori_loop(1, bricks, sent, 0)

    def settle(d, carry):
        for e in range(1, mem_count):
            to_member(d, e).wait()
        return carry

    lax.fori_loop(0, bricks, settle, 0)


def update_kernel(count_ref, slot_ref, tile_ref, recv_ref, model_ref, members_ref, out_ref):
    foot = tile_ref.shape[0]
    block = members_ref.shape[0]
    cap = slot_ref.shape[0] // recv_ref.shape[0]
    total = count_ref[0]
    out_ref[...] = members_ref[...]

    def turn(step, carry):
        results = []
        for u in range(GROUP):
            at = step * GROUP + u
            owner = slot_ref[at] // cap
            rank = slot_ref[at] % cap
            weight = recv_ref[owner, pl.ds(pl.multiple_of(rank * block, block), block), :]
            taper = recv_ref[owner, cap * block : cap * (block + foot), :]
            taper = taper.astype(jnp.float32).reshape(cap, foot, 128)
            mine = lax.broadcasted_iota(jnp.int32, (cap, foot, 128), 0) == rank
            taper = jnp.sum(jnp.where(mine, taper, 0.0), axis=0)
            used = at < total
            for c in range(foot):
                start = pl.multiple_of(tile_ref[c, at] * 128, 128)
                part = jnp.dot(
                    weight, model_ref[:, pl.ds(start, 128)], preferred_element_type=jnp.float32
                )
                results.append((start, jnp.where(used, part * taper[c : c + 1], 0.0)))
        for start, part in results:
            out_ref[:, pl.ds(start, 128)] += part
        return carry

    lax.fori_loop(0, (total + GROUP - 1) // GROUP, turn, 0)


def body(
    members, predicted, perturbation, observed, noise_std, taper_weights, foot_brick, foot_tiles
):
    mem_count = lax.axis_size("mem")
    brick_count = lax.axis_size("brick")
    part, gates, wide = predicted.shape
    ensemble = part * brick_count
    local = wide // brick_count
    block = ensemble // mem_count
    foot = foot_tiles.shape[1]
    foot_length = taper_weights.shape[1]
    devices = mem_count * brick_count
    cap = max(2, 2 * local // brick_count)
    slots = devices * cap
    vmem = pltpu.CompilerParams(vmem_limit_bytes=48 * 1024 * 1024)
    in_vmem = pl.BlockSpec(memory_space=pltpu.VMEM)
    in_smem = pl.BlockSpec(memory_space=pltpu.SMEM)

    model_all = lax.all_gather(members.astype(jnp.bfloat16), "mem", axis=0, tiled=True)

    pair = jnp.concatenate([predicted, perturbation], axis=1).astype(jnp.bfloat16)
    pair = jnp.transpose(pair, (2, 0, 1))
    pair = jnp.pad(pair, ((0, 0), (0, 0), (0, 128 - 2 * gates)))
    pair = pair.reshape(brick_count, local, part, 128)
    data = lax.all_to_all(pair, "brick", split_axis=0, concat_axis=0, tiled=True)

    destination = foot_brick[:, 0]
    order = jnp.arange(local)
    before = order[None, :] < order[:, None]
    rank = jnp.sum(
        ((destination[:, None] == destination[None, :]) & before).astype(jnp.int32), axis=1
    )
    slot_of = destination * cap + rank
    hot = slot_of[None, :] == jnp.arange(brick_count * cap, dtype=jnp.int32)[:, None]
    index = jnp.sum(jnp.where(hot, order[None, :], 0), axis=1)
    numbers = jnp.concatenate([foot_tiles, jnp.ones((local, 1), jnp.int32)], axis=1)
    numbers = jnp.pad(numbers.astype(jnp.bfloat16), ((0, 0), (0, 127 - foot)))
    extra = jnp.concatenate([taper_weights, numbers], axis=1)
    extra = jnp.dot(hot.astype(jnp.bfloat16), extra, preferred_element_type=jnp.float32)
    extra = extra.astype(jnp.bfloat16)
    taper_slots = extra[:, :foot_length].reshape(brick_count, cap * foot, 128)
    number_slots = extra[:, foot_length:].reshape(brick_count, cap, 128)
    tail = -(-cap * (foot + 1) // 16) * 16
    taper_slots = jnp.concatenate([taper_slots, number_slots], axis=1)
    taper_slots = jnp.pad(taper_slots, ((0, 0), (0, tail - cap * (foot + 1)), (0, 0)))

    fact = pl.pallas_call(
        factor_kernel,
        out_shape=jax.ShapeDtypeStruct((local, 2 * gates, ensemble), jnp.bfloat16),
        in_specs=[in_vmem] * 3,
        out_specs=in_vmem,
        scratch_shapes=[
            pltpu.VMEM((local, gates, ensemble), jnp.float32),
            pltpu.VMEM((local, gates, ensemble), jnp.float32),
            pltpu.VMEM((local, gates, gates), jnp.float32),
            pltpu.VMEM((gates, gates, local), jnp.float32),
            pltpu.VMEM((local, gates, gates), jnp.float32),
        ],
        compiler_params=vmem,
        cost_estimate=pl.CostEstimate(flops=400_000_000, bytes_accessed=5_000_000, transcendentals=0),
    )(data, jnp.transpose(observed)[:, :, None], jnp.transpose(noise_std)[:, :, None])

    packed_rows = cap * 2 * gates + tail
    out_rows = cap * block + tail
    recv = pl.pallas_call(
        exchange_kernel,
        out_shape=jax.ShapeDtypeStruct((mem_count, brick_count, out_rows, 128), jnp.bfloat16),
        in_specs=[in_smem] + [in_vmem] * 2,
        out_specs=in_vmem,
        scratch_shapes=[
            pltpu.VMEM((brick_count, packed_rows, 128), jnp.bfloat16),
            pltpu.VMEM((brick_count, packed_rows, 128), jnp.bfloat16),
            pltpu.VMEM((brick_count, mem_count, out_rows, 128), jnp.bfloat16),
            pltpu.SemaphoreType.DMA((brick_count,)),
            pltpu.SemaphoreType.DMA((brick_count,)),
            pltpu.SemaphoreType.DMA((brick_count * mem_count,)),
            pltpu.SemaphoreType.DMA((brick_count * mem_count,)),
        ],
        compiler_params=pltpu.CompilerParams(
            vmem_limit_bytes=48 * 1024 * 1024, collective_id=0, has_side_effects=True
        ),
        cost_estimate=pl.CostEstimate(flops=100_000_000, bytes_accessed=8_000_000, transcendentals=0),
    )(index, fact, taper_slots).reshape(devices, out_rows, 128)

    numbers = recv[:, cap * (block + foot) : cap * (block + foot + 1), : foot + 1]
    numbers = numbers.astype(jnp.float32).astype(jnp.int32).reshape(slots, foot + 1)
    filled = numbers[:, foot] == 1
    spots = jnp.arange(slots)
    position = jnp.sum((filled[None, :] & (spots[None, :] < spots[:, None])).astype(jnp.int32), axis=1)
    listed = filled[None, :] & (position[None, :] == spots[:, None])
    slot_list = jnp.sum(jnp.where(listed, spots[None, :], 0), axis=1)
    tile_list = jnp.sum(
        jnp.where(listed[None], jnp.transpose(numbers[:, :foot])[:, None, :], 0), axis=2
    )
    count = jnp.sum(filled.astype(jnp.int32)).reshape(1)

    return pl.pallas_call(
        update_kernel,
        out_shape=jax.ShapeDtypeStruct(members.shape, members.dtype),
        in_specs=[in_smem] * 3 + [in_vmem] * 3,
        out_specs=in_vmem,
        compiler_params=vmem,
        cost_estimate=pl.CostEstimate(flops=600_000_000, bytes_accessed=10_000_000, transcendentals=0),
    )(count, slot_list, tile_list, recv, model_all, members)


def solution(mesh):
    in_specs = (
        P("mem", "brick"),
        P("brick", None, "mem"),
        P("brick", None, "mem"),
        P(None, ("mem", "brick")),
        P(None, ("mem", "brick")),
        P(("mem", "brick"), None),
        P(("mem", "brick"), None),
        P(("mem", "brick"), None),
    )
    out_specs = P("mem", "brick")
    return jax.shard_map(body, mesh=mesh, in_specs=in_specs, out_specs=out_specs, check_vma=False)
```

```python
import jax
import jax.numpy as jnp
from jax import lax
from jax.experimental import pallas as pl
from jax.experimental.pallas import tpu as pltpu
from jax.sharding import PartitionSpec as P

GROUP = 4
HIGH = lax.Precision.HIGHEST


def owner_kernel(
    index_ref,
    pair_ref,
    obs_ref,
    std_ref,
    taper_ref,
    out_ref,
    data,
    anom,
    misf,
    cov,
    work,
    inv,
    stage_a,
    stage_g,
    landed_a,
    landed_g,
    spread,
    p_send,
    p_recv,
    a_send,
    a_recv,
    g_send,
    g_recv,
    m_send,
    m_recv,
):
    mem_count, bricks, out_rows, _ = out_ref.shape
    _, soundings, part, lanes = pair_ref.shape
    ensemble = bricks * part
    gates = obs_ref.shape[1]
    tail = taper_ref.shape[1]
    cap = index_ref.shape[0] // bricks
    block = (out_rows - tail) // cap
    held_rows = cap * gates
    at_m = lax.axis_index("mem")
    at_b = lax.axis_index("brick")
    mesh_ids = pl.DeviceIdType.MESH

    barrier = pltpu.get_barrier_semaphore()
    for d in range(1, bricks):
        pl.semaphore_signal(
            barrier, inc=1, device_id=(at_m, lax.rem(at_b + d, bricks)), device_id_type=mesh_ids
        )
    for e in range(1, mem_count):
        pl.semaphore_signal(
            barrier, inc=1, device_id=(lax.rem(at_m + e, mem_count), at_b), device_id_type=mesh_ids
        )
    pl.semaphore_wait(barrier, bricks + mem_count - 2)

    def along_brick(d, source, target, send_sem, recv_sem):
        there = lax.rem(at_b + d, bricks)
        return pltpu.make_async_remote_copy(
            src_ref=source.at[there],
            dst_ref=target.at[at_b],
            send_sem=send_sem.at[d],
            recv_sem=recv_sem.at[d],
            device_id=(at_m, there),
            device_id_type=mesh_ids,
        )

    def send_pair(d):
        return along_brick(d, pair_ref, data, p_send, p_recv)

    def send_anomaly(d):
        return along_brick(d, stage_a, landed_a, a_send, a_recv)

    def send_gain(d):
        return along_brick(d, stage_g, landed_g, g_send, g_recv)

    def to_member(d, e):
        source = lax.rem(at_b - d + bricks, bricks)
        there = lax.rem(at_m + e, mem_count)
        return pltpu.make_async_remote_copy(
            src_ref=spread.at[source, there],
            dst_ref=out_ref.at[at_m, source],
            send_sem=m_send.at[d * mem_count + e],
            recv_sem=m_recv.at[d * mem_count + e],
            device_id=(there, at_b),
            device_id_type=mesh_ids,
        )

    def each_peer(step):
        def turn(d, carry):
            step(d)
            return carry

        lax.fori_loop(1, bricks, turn, 0)

    each_peer(lambda d: send_pair(d).start())
    data[at_b] = pair_ref[at_b]
    each_peer(lambda d: send_pair(d).wait())

    row = lax.broadcasted_iota(jnp.int32, (gates, gates), 0)
    column = lax.broadcasted_iota(jnp.int32, (gates, gates), 1)

    def prepare(s, carry):
        turned = data[:, s].astype(jnp.float32).reshape(ensemble, lanes).T
        pred = turned[:gates]
        pert = turned[gates : 2 * gates]
        std = std_ref[s]
        anomaly = pred - jnp.sum(pred, axis=1, keepdims=True) / ensemble
        misf[s] = obs_ref[s] + std * pert - pred
        anom[s] = anomaly
        total = lax.dot_general(
            anomaly,
            anomaly,
            (((1,), (1,)), ((), ())),
            precision=HIGH,
            preferred_element_type=jnp.float32,
        ) / (ensemble - 1.0)
        cov[s] = total + jnp.where(row == column, std * std, 0.0)
        return carry

    lax.fori_loop(0, soundings, prepare, 0, unroll=2)

    def pack(values, ref, place, there):
        for r in range(0, cap, 2):
            first = values[index_ref[there * cap + r]]
            second = values[index_ref[there * cap + r + 1]]
            both = jnp.concatenate([first, second], axis=0).astype(jnp.bfloat16)
            ref[place, pl.ds(r * gates, 2 * gates), :] = both

    def post_anomaly(d):
        there = lax.rem(at_b + d, bricks)
        pack(anom, stage_a, there, there)
        stage_a[there, pl.ds(held_rows, tail), :] = taper_ref[there]
        send_anomaly(d).start()

    each_peer(post_anomaly)
    pack(anom, landed_a, at_b, at_b)
    landed_a[at_b, pl.ds(held_rows, tail), :] = taper_ref[at_b]

    for i in range(gates):
        work[i] = cov[:, i, :].T

    place = lax.broadcasted_iota(jnp.int32, (gates, soundings), 0)

    def sweep(k, carry):
        scale = 1.0 / work[k, pl.ds(k, 1), :]
        pivot = work[k]
        scaled = jnp.where(place == k, scale, pivot * scale)
        kept = jnp.where(place == k, 0.0, 1.0)
        for i in range(gates):
            coef = work[i, pl.ds(k, 1), :]
            work[i] = work[i] * kept - coef * scaled
        work[k] = scaled
        return carry

    lax.fori_loop(0, gates, sweep, 0)

    for i in range(gates):
        inv[:, i, :] = work[i].T

    def finish(s, carry):
        misf[s] = lax.dot_general(
            inv[s],
            misf[s],
            (((1,), (0,)), ((), ())),
            precision=HIGH,
            preferred_element_type=jnp.float32,
        ) / (ensemble - 1.0)
        return carry

    lax.fori_loop(0, soundings, finish, 0, unroll=4)

    def post_gain(d):
        there = lax.rem(at_b + d, bricks)
        pack(misf, stage_g, there, there)
        send_gain(d).start()

    each_peer(post_gain)
    pack(misf, landed_g, at_b, at_b)

    def weigh(d):
        source = lax.rem(at_b - d + bricks, bricks)
        for r in range(0, cap, 2):
            gains = landed_g[source, pl.ds(r * gates, 2 * gates), :].astype(jnp.float32)
            anomalies = landed_a[source, pl.ds(r * gates, 2 * gates), :].astype(jnp.float32)
            for h in range(2):
                weight = jnp.dot(
                    gains[h * gates : (h + 1) * gates].T.astype(jnp.bfloat16),
                    anomalies[h * gates : (h + 1) * gates].astype(jnp.bfloat16),
                    preferred_element_type=jnp.float32,
                ).astype(jnp.bfloat16)
                for m in range(mem_count):
                    spread[source, m, pl.ds((r + h) * block, block), :] = weight[
                        m * block : (m + 1) * block
                    ]
        tapers = landed_a[source, pl.ds(held_rows, tail), :]
        for m in range(mem_count):
            spread[source, m, pl.ds(cap * block, tail), :] = tapers
        for e in range(1, mem_count):
            to_member(d, e).start()
        out_ref[at_m, source] = spread[source, at_m]

    weigh(0)

    def take(d):
        send_anomaly(d).wait_recv()
        send_gain(d).wait_recv()
        weigh(d)

    each_peer(take)

    def sent(d):
        send_anomaly(d).wait_send()
        send_gain(d).wait_send()

    each_peer(sent)

    def settle(d, carry):
        for e in range(1, mem_count):
            to_member(d, e).wait()
        return carry

    lax.fori_loop(0, bricks, settle, 0)


def update_kernel(count_ref, slot_ref, tile_ref, recv_ref, model_ref, members_ref, out_ref):
    foot = tile_ref.shape[0]
    block = members_ref.shape[0]
    cap = slot_ref.shape[0] // recv_ref.shape[0]
    total = count_ref[0]
    out_ref[...] = members_ref[...]

    def turn(step, carry):
        results = []
        for u in range(GROUP):
            at = step * GROUP + u
            owner = slot_ref[at] // cap
            rank = slot_ref[at] % cap
            weight = recv_ref[owner, pl.ds(pl.multiple_of(rank * block, block), block), :]
            taper = recv_ref[owner, cap * block : cap * (block + foot), :]
            taper = taper.astype(jnp.float32).reshape(cap, foot, 128)
            mine = lax.broadcasted_iota(jnp.int32, (cap, foot, 128), 0) == rank
            taper = jnp.sum(jnp.where(mine, taper, 0.0), axis=0)
            used = at < total
            for c in range(foot):
                start = pl.multiple_of(tile_ref[c, at] * 128, 128)
                part = jnp.dot(
                    weight, model_ref[:, pl.ds(start, 128)], preferred_element_type=jnp.float32
                )
                results.append((start, jnp.where(used, part * taper[c : c + 1], 0.0)))
        for start, part in results:
            out_ref[:, pl.ds(start, 128)] += part
        return carry

    lax.fori_loop(0, (total + GROUP - 1) // GROUP, turn, 0)


def body(
    members, predicted, perturbation, observed, noise_std, taper_weights, foot_brick, foot_tiles
):
    mem_count = lax.axis_size("mem")
    brick_count = lax.axis_size("brick")
    part, gates, wide = predicted.shape
    ensemble = part * brick_count
    local = wide // brick_count
    block = ensemble // mem_count
    foot = foot_tiles.shape[1]
    foot_length = taper_weights.shape[1]
    devices = mem_count * brick_count
    cap = max(2, 2 * local // brick_count)
    slots = devices * cap
    vmem = pltpu.CompilerParams(vmem_limit_bytes=48 * 1024 * 1024)
    in_vmem = pl.BlockSpec(memory_space=pltpu.VMEM)
    in_smem = pl.BlockSpec(memory_space=pltpu.SMEM)

    model_all = lax.all_gather(members.astype(jnp.bfloat16), "mem", axis=0, tiled=True)

    pair = jnp.concatenate([predicted, perturbation], axis=1).astype(jnp.bfloat16)
    pair = jnp.transpose(pair, (2, 0, 1))
    pair = jnp.pad(pair, ((0, 0), (0, 0), (0, 128 - 2 * gates)))
    pair = pair.reshape(brick_count, local, part, 128)
    destination = foot_brick[:, 0]
    order = jnp.arange(local)
    before = order[None, :] < order[:, None]
    rank = jnp.sum(
        ((destination[:, None] == destination[None, :]) & before).astype(jnp.int32), axis=1
    )
    slot_of = destination * cap + rank
    hot = slot_of[None, :] == jnp.arange(brick_count * cap, dtype=jnp.int32)[:, None]
    index = jnp.sum(jnp.where(hot, order[None, :], 0), axis=1)
    numbers = jnp.concatenate([foot_tiles, jnp.ones((local, 1), jnp.int32)], axis=1)
    numbers = jnp.pad(numbers.astype(jnp.bfloat16), ((0, 0), (0, 127 - foot)))
    extra = jnp.concatenate([taper_weights, numbers], axis=1)
    extra = jnp.dot(hot.astype(jnp.bfloat16), extra, preferred_element_type=jnp.float32)
    extra = extra.astype(jnp.bfloat16)
    taper_slots = extra[:, :foot_length].reshape(brick_count, cap * foot, 128)
    number_slots = extra[:, foot_length:].reshape(brick_count, cap, 128)
    tail = -(-cap * (foot + 1) // 16) * 16
    taper_slots = jnp.concatenate([taper_slots, number_slots], axis=1)
    taper_slots = jnp.pad(taper_slots, ((0, 0), (0, tail - cap * (foot + 1)), (0, 0)))

    out_rows = cap * block + tail
    recv = pl.pallas_call(
        owner_kernel,
        out_shape=jax.ShapeDtypeStruct((mem_count, brick_count, out_rows, 128), jnp.bfloat16),
        in_specs=[in_smem] + [in_vmem] * 4,
        out_specs=in_vmem,
        scratch_shapes=[
            pltpu.VMEM(pair.shape, jnp.bfloat16),
            pltpu.VMEM((local, gates, ensemble), jnp.float32),
            pltpu.VMEM((local, gates, ensemble), jnp.float32),
            pltpu.VMEM((local, gates, gates), jnp.float32),
            pltpu.VMEM((gates, gates, local), jnp.float32),
            pltpu.VMEM((local, gates, gates), jnp.float32),
            pltpu.VMEM((brick_count, cap * gates + tail, 128), jnp.bfloat16),
            pltpu.VMEM((brick_count, cap * gates, 128), jnp.bfloat16),
            pltpu.VMEM((brick_count, cap * gates + tail, 128), jnp.bfloat16),
            pltpu.VMEM((brick_count, cap * gates, 128), jnp.bfloat16),
            pltpu.VMEM((brick_count, mem_count, out_rows, 128), jnp.bfloat16),
        ]
        + [pltpu.SemaphoreType.DMA((brick_count,))] * 6
        + [pltpu.SemaphoreType.DMA((brick_count * mem_count,))] * 2,
        compiler_params=pltpu.CompilerParams(
            vmem_limit_bytes=48 * 1024 * 1024, collective_id=0, has_side_effects=True
        ),
        cost_estimate=pl.CostEstimate(
            flops=20_000_000_000, bytes_accessed=200_000_000, transcendentals=0
        ),
    )(
        index,
        pair,
        jnp.transpose(observed)[:, :, None],
        jnp.transpose(noise_std)[:, :, None],
        taper_slots,
    ).reshape(devices, out_rows, 128)

    numbers = recv[:, cap * (block + foot) : cap * (block + foot + 1), : foot + 1]
    numbers = numbers.astype(jnp.float32).astype(jnp.int32).reshape(slots, foot + 1)
    filled = numbers[:, foot] == 1
    spots = jnp.arange(slots)
    position = jnp.sum((filled[None, :] & (spots[None, :] < spots[:, None])).astype(jnp.int32), axis=1)
    listed = filled[None, :] & (position[None, :] == spots[:, None])
    slot_list = jnp.sum(jnp.where(listed, spots[None, :], 0), axis=1)
    tile_list = jnp.sum(
        jnp.where(listed[None], jnp.transpose(numbers[:, :foot])[:, None, :], 0), axis=2
    )
    count = jnp.sum(filled.astype(jnp.int32)).reshape(1)

    return pl.pallas_call(
        update_kernel,
        out_shape=jax.ShapeDtypeStruct(members.shape, members.dtype),
        in_specs=[in_smem] * 3 + [in_vmem] * 3,
        out_specs=in_vmem,
        compiler_params=vmem,
        cost_estimate=pl.CostEstimate(flops=600_000_000, bytes_accessed=10_000_000, transcendentals=0),
    )(count, slot_list, tile_list, recv, model_all, members)


def solution(mesh):
    in_specs = (
        P("mem", "brick"),
        P("brick", None, "mem"),
        P("brick", None, "mem"),
        P(None, ("mem", "brick")),
        P(None, ("mem", "brick")),
        P(("mem", "brick"), None),
        P(("mem", "brick"), None),
        P(("mem", "brick"), None),
    )
    out_specs = P("mem", "brick")
    return jax.shard_map(body, mesh=mesh, in_specs=in_specs, out_specs=out_specs, check_vma=False)
```

```python
import jax
import jax.numpy as jnp
from jax import lax
from jax.experimental import pallas as pl
from jax.experimental.pallas import tpu as pltpu
from jax.sharding import PartitionSpec as P

GROUP = 4
PIECES = 4
HIGH = lax.Precision.HIGHEST


def owner_kernel(
    index_ref,
    pair_ref,
    obs_ref,
    std_ref,
    taper_ref,
    out_ref,
    data,
    anom,
    misf,
    cov,
    work,
    inv,
    stage_a,
    stage_g,
    landed_a,
    landed_g,
    spread,
    p_send,
    p_recv,
    a_send,
    a_recv,
    g_send,
    g_recv,
    m_send,
    m_recv,
):
    mem_count, bricks, out_rows, _ = out_ref.shape
    _, soundings, part, lanes = pair_ref.shape
    ensemble = bricks * part
    gates = obs_ref.shape[1]
    tail = taper_ref.shape[1]
    cap = index_ref.shape[0] // bricks
    block = (out_rows - tail) // cap
    held_rows = cap * gates
    at_m = lax.axis_index("mem")
    at_b = lax.axis_index("brick")
    mesh_ids = pl.DeviceIdType.MESH

    barrier = pltpu.get_barrier_semaphore()
    for d in range(1, bricks):
        pl.semaphore_signal(
            barrier, inc=1, device_id=(at_m, lax.rem(at_b + d, bricks)), device_id_type=mesh_ids
        )
    for e in range(1, mem_count):
        pl.semaphore_signal(
            barrier, inc=1, device_id=(lax.rem(at_m + e, mem_count), at_b), device_id_type=mesh_ids
        )
    pl.semaphore_wait(barrier, bricks + mem_count - 2)

    def along_brick(d, source, target, send_sem, recv_sem):
        there = lax.rem(at_b + d, bricks)
        return pltpu.make_async_remote_copy(
            src_ref=source.at[there],
            dst_ref=target.at[at_b],
            send_sem=send_sem.at[d],
            recv_sem=recv_sem.at[d],
            device_id=(at_m, there),
            device_id_type=mesh_ids,
        )

    piece = soundings // PIECES

    def send_pair(d, h):
        there = lax.rem(at_b + d, bricks)
        return pltpu.make_async_remote_copy(
            src_ref=pair_ref.at[there, pl.ds(h * piece, piece)],
            dst_ref=data.at[at_b, pl.ds(h * piece, piece)],
            send_sem=p_send.at[h * bricks + d],
            recv_sem=p_recv.at[h * bricks + d],
            device_id=(at_m, there),
            device_id_type=mesh_ids,
        )

    def send_anomaly(d):
        return along_brick(d, stage_a, landed_a, a_send, a_recv)

    def send_gain(d):
        return along_brick(d, stage_g, landed_g, g_send, g_recv)

    def to_member(d, e):
        source = lax.rem(at_b - d + bricks, bricks)
        there = lax.rem(at_m + e, mem_count)
        return pltpu.make_async_remote_copy(
            src_ref=spread.at[source, there],
            dst_ref=out_ref.at[at_m, source],
            send_sem=m_send.at[d * mem_count + e],
            recv_sem=m_recv.at[d * mem_count + e],
            device_id=(there, at_b),
            device_id_type=mesh_ids,
        )

    def each_peer(step):
        def turn(d, carry):
            step(d)
            return carry

        lax.fori_loop(1, bricks, turn, 0)

    for h in range(PIECES):
        each_peer(lambda d: send_pair(d, h).start())
    data[at_b] = pair_ref[at_b]

    row = lax.broadcasted_iota(jnp.int32, (gates, gates), 0)
    column = lax.broadcasted_iota(jnp.int32, (gates, gates), 1)

    def prepare(s, carry):
        turned = data[:, s].astype(jnp.float32).reshape(ensemble, lanes).T
        pred = turned[:gates]
        pert = turned[gates : 2 * gates]
        std = std_ref[s]
        anomaly = pred - jnp.sum(pred, axis=1, keepdims=True) / ensemble
        misf[s] = obs_ref[s] + std * pert - pred
        anom[s] = anomaly
        total = lax.dot_general(
            anomaly,
            anomaly,
            (((1,), (1,)), ((), ())),
            precision=HIGH,
            preferred_element_type=jnp.float32,
        ) / (ensemble - 1.0)
        cov[s] = total + jnp.where(row == column, std * std, 0.0)
        return carry

    for h in range(PIECES):
        each_peer(lambda d: send_pair(d, h).wait())
        lax.fori_loop(h * piece, (h + 1) * piece, prepare, 0, unroll=4)

    def pack(values, ref, place, there):
        for r in range(0, cap, 2):
            first = values[index_ref[there * cap + r]]
            second = values[index_ref[there * cap + r + 1]]
            both = jnp.concatenate([first, second], axis=0).astype(jnp.bfloat16)
            ref[place, pl.ds(r * gates, 2 * gates), :] = both

    def post_anomaly(d):
        there = lax.rem(at_b + d, bricks)
        pack(anom, stage_a, there, there)
        stage_a[there, pl.ds(held_rows, tail), :] = taper_ref[there]
        send_anomaly(d).start()

    each_peer(post_anomaly)
    pack(anom, landed_a, at_b, at_b)
    landed_a[at_b, pl.ds(held_rows, tail), :] = taper_ref[at_b]

    for i in range(gates):
        work[i] = cov[:, i, :].T

    place = lax.broadcasted_iota(jnp.int32, (gates, soundings), 0)

    def sweep(k, carry):
        scale = 1.0 / work[k, pl.ds(k, 1), :]
        pivot = work[k]
        scaled = jnp.where(place == k, scale, pivot * scale)
        kept = jnp.where(place == k, 0.0, 1.0)
        for i in range(gates):
            coef = work[i, pl.ds(k, 1), :]
            work[i] = work[i] * kept - coef * scaled
        work[k] = scaled
        return carry

    lax.fori_loop(0, gates, sweep, 0)

    for i in range(gates):
        inv[:, i, :] = work[i].T

    def finish(s, carry):
        misf[s] = lax.dot_general(
            inv[s],
            misf[s],
            (((1,), (0,)), ((), ())),
            precision=HIGH,
            preferred_element_type=jnp.float32,
        ) / (ensemble - 1.0)
        return carry

    lax.fori_loop(0, soundings, finish, 0, unroll=4)

    def post_gain(d):
        there = lax.rem(at_b + d, bricks)
        pack(misf, stage_g, there, there)
        send_gain(d).start()

    each_peer(post_gain)
    pack(misf, landed_g, at_b, at_b)

    def weigh(d):
        source = lax.rem(at_b - d + bricks, bricks)
        for r in range(0, cap, 2):
            gains = landed_g[source, pl.ds(r * gates, 2 * gates), :].astype(jnp.float32)
            anomalies = landed_a[source, pl.ds(r * gates, 2 * gates), :].astype(jnp.float32)
            for h in range(2):
                weight = jnp.dot(
                    gains[h * gates : (h + 1) * gates].T.astype(jnp.bfloat16),
                    anomalies[h * gates : (h + 1) * gates].astype(jnp.bfloat16),
                    preferred_element_type=jnp.float32,
                ).astype(jnp.bfloat16)
                for m in range(mem_count):
                    spread[source, m, pl.ds((r + h) * block, block), :] = weight[
                        m * block : (m + 1) * block
                    ]
        tapers = landed_a[source, pl.ds(held_rows, tail), :]
        for m in range(mem_count):
            spread[source, m, pl.ds(cap * block, tail), :] = tapers
        for e in range(1, mem_count):
            to_member(d, e).start()
        out_ref[at_m, source] = spread[source, at_m]

    weigh(0)

    def take(d):
        send_anomaly(d).wait_recv()
        send_gain(d).wait_recv()
        weigh(d)

    each_peer(take)

    def sent(d):
        send_anomaly(d).wait_send()
        send_gain(d).wait_send()

    each_peer(sent)

    def settle(d, carry):
        for e in range(1, mem_count):
            to_member(d, e).wait()
        return carry

    lax.fori_loop(0, bricks, settle, 0)


def update_kernel(
    count_ref, slot_ref, tile_ref, recv_ref, model_ref, members_ref, out_ref, tapers
):
    foot = tile_ref.shape[0]
    block = members_ref.shape[0]
    cap = slot_ref.shape[0] // recv_ref.shape[0]
    total = count_ref[0]
    out_ref[...] = members_ref[...]
    tapers[...] = recv_ref[:, cap * block : cap * (block + foot), :].astype(jnp.float32)

    def turn(step, carry):
        results = []
        for u in range(GROUP):
            at = step * GROUP + u
            owner = slot_ref[at] // cap
            rank = slot_ref[at] % cap
            weight = recv_ref[owner, pl.ds(pl.multiple_of(rank * block, block), block), :]
            used = at < total
            starts = [pl.multiple_of(tile_ref[c, at] * 128, 128) for c in range(foot)]
            cells = jnp.concatenate([model_ref[:, pl.ds(start, 128)] for start in starts], axis=1)
            part = jnp.dot(weight, cells, preferred_element_type=jnp.float32)
            for c, start in enumerate(starts):
                taper = tapers[owner, pl.ds(rank * foot + c, 1), :]
                scaled = part[:, c * 128 : (c + 1) * 128] * taper
                results.append((start, jnp.where(used, scaled, 0.0)))
        for start, scaled in results:
            out_ref[:, pl.ds(start, 128)] += scaled
        return carry

    lax.fori_loop(0, (total + GROUP - 1) // GROUP, turn, 0)


def body(
    members, predicted, perturbation, observed, noise_std, taper_weights, foot_brick, foot_tiles
):
    mem_count = lax.axis_size("mem")
    brick_count = lax.axis_size("brick")
    part, gates, wide = predicted.shape
    ensemble = part * brick_count
    local = wide // brick_count
    block = ensemble // mem_count
    foot = foot_tiles.shape[1]
    foot_length = taper_weights.shape[1]
    devices = mem_count * brick_count
    cap = max(2, 2 * local // brick_count)
    slots = devices * cap
    vmem = pltpu.CompilerParams(vmem_limit_bytes=48 * 1024 * 1024)
    in_vmem = pl.BlockSpec(memory_space=pltpu.VMEM)
    in_smem = pl.BlockSpec(memory_space=pltpu.SMEM)

    model_all = lax.all_gather(members.astype(jnp.bfloat16), "mem", axis=0, tiled=True)

    pair = jnp.concatenate([predicted, perturbation], axis=1).astype(jnp.bfloat16)
    pair = jnp.transpose(pair, (2, 0, 1))
    pair = jnp.pad(pair, ((0, 0), (0, 0), (0, 128 - 2 * gates)))
    pair = pair.reshape(brick_count, local, part, 128)
    destination = foot_brick[:, 0]
    order = jnp.arange(local)
    before = order[None, :] < order[:, None]
    rank = jnp.sum(
        ((destination[:, None] == destination[None, :]) & before).astype(jnp.int32), axis=1
    )
    slot_of = destination * cap + rank
    hot = slot_of[None, :] == jnp.arange(brick_count * cap, dtype=jnp.int32)[:, None]
    index = jnp.sum(jnp.where(hot, order[None, :], 0), axis=1)
    numbers = jnp.concatenate([foot_tiles, jnp.ones((local, 1), jnp.int32)], axis=1)
    numbers = jnp.pad(numbers.astype(jnp.bfloat16), ((0, 0), (0, 127 - foot)))
    extra = jnp.concatenate([taper_weights, numbers], axis=1)
    extra = jnp.dot(hot.astype(jnp.bfloat16), extra, preferred_element_type=jnp.float32)
    extra = extra.astype(jnp.bfloat16)
    taper_slots = extra[:, :foot_length].reshape(brick_count, cap * foot, 128)
    number_slots = extra[:, foot_length:].reshape(brick_count, cap, 128)
    tail = -(-cap * (foot + 1) // 16) * 16
    taper_slots = jnp.concatenate([taper_slots, number_slots], axis=1)
    taper_slots = jnp.pad(taper_slots, ((0, 0), (0, tail - cap * (foot + 1)), (0, 0)))

    out_rows = cap * block + tail
    recv = pl.pallas_call(
        owner_kernel,
        out_shape=jax.ShapeDtypeStruct((mem_count, brick_count, out_rows, 128), jnp.bfloat16),
        in_specs=[in_smem] + [in_vmem] * 4,
        out_specs=in_vmem,
        scratch_shapes=[
            pltpu.VMEM(pair.shape, jnp.bfloat16),
            pltpu.VMEM((local, gates, ensemble), jnp.float32),
            pltpu.VMEM((local, gates, ensemble), jnp.float32),
            pltpu.VMEM((local, gates, gates), jnp.float32),
            pltpu.VMEM((gates, gates, local), jnp.float32),
            pltpu.VMEM((local, gates, gates), jnp.float32),
            pltpu.VMEM((brick_count, cap * gates + tail, 128), jnp.bfloat16),
            pltpu.VMEM((brick_count, cap * gates, 128), jnp.bfloat16),
            pltpu.VMEM((brick_count, cap * gates + tail, 128), jnp.bfloat16),
            pltpu.VMEM((brick_count, cap * gates, 128), jnp.bfloat16),
            pltpu.VMEM((brick_count, mem_count, out_rows, 128), jnp.bfloat16),
        ]
        + [pltpu.SemaphoreType.DMA((brick_count * PIECES,))] * 2
        + [pltpu.SemaphoreType.DMA((brick_count,))] * 4
        + [pltpu.SemaphoreType.DMA((brick_count * mem_count,))] * 2,
        compiler_params=pltpu.CompilerParams(
            vmem_limit_bytes=48 * 1024 * 1024, collective_id=0, has_side_effects=True
        ),
        cost_estimate=pl.CostEstimate(
            flops=20_000_000_000, bytes_accessed=200_000_000, transcendentals=0
        ),
    )(
        index,
        pair,
        jnp.transpose(observed)[:, :, None],
        jnp.transpose(noise_std)[:, :, None],
        taper_slots,
    ).reshape(devices, out_rows, 128)

    numbers = recv[:, cap * (block + foot) : cap * (block + foot + 1), : foot + 1]
    numbers = numbers.astype(jnp.float32).astype(jnp.int32).reshape(slots, foot + 1)
    filled = numbers[:, foot] == 1
    spots = jnp.arange(slots)
    position = jnp.sum((filled[None, :] & (spots[None, :] < spots[:, None])).astype(jnp.int32), axis=1)
    listed = filled[None, :] & (position[None, :] == spots[:, None])
    slot_list = jnp.sum(jnp.where(listed, spots[None, :], 0), axis=1)
    tile_list = jnp.sum(
        jnp.where(listed[None], jnp.transpose(numbers[:, :foot])[:, None, :], 0), axis=2
    )
    count = jnp.sum(filled.astype(jnp.int32)).reshape(1)

    return pl.pallas_call(
        update_kernel,
        out_shape=jax.ShapeDtypeStruct(members.shape, members.dtype),
        in_specs=[in_smem] * 3 + [in_vmem] * 3,
        out_specs=in_vmem,
        scratch_shapes=[pltpu.VMEM((devices, cap * foot, 128), jnp.float32)],
        compiler_params=vmem,
        cost_estimate=pl.CostEstimate(flops=600_000_000, bytes_accessed=10_000_000, transcendentals=0),
    )(count, slot_list, tile_list, recv, model_all, members)


def solution(mesh):
    in_specs = (
        P("mem", "brick"),
        P("brick", None, "mem"),
        P("brick", None, "mem"),
        P(None, ("mem", "brick")),
        P(None, ("mem", "brick")),
        P(("mem", "brick"), None),
        P(("mem", "brick"), None),
        P(("mem", "brick"), None),
    )
    out_specs = P("mem", "brick")
    return jax.shard_map(body, mesh=mesh, in_specs=in_specs, out_specs=out_specs, check_vma=False)
```

```python
import jax
import jax.numpy as jnp
from jax import lax
from jax.experimental import pallas as pl
from jax.experimental.pallas import tpu as pltpu
from jax.sharding import PartitionSpec as P

GROUP = 8
PIECES = 4
HIGH = lax.Precision.HIGHEST


def owner_kernel(
    index_ref,
    pair_ref,
    obs_ref,
    std_ref,
    taper_ref,
    out_ref,
    data,
    anom,
    misf,
    cov,
    work,
    inv,
    stage_a,
    stage_g,
    landed_a,
    landed_g,
    spread,
    p_send,
    p_recv,
    a_send,
    a_recv,
    g_send,
    g_recv,
    m_send,
    m_recv,
):
    mem_count, bricks, out_rows, _ = out_ref.shape
    _, soundings, part, lanes = pair_ref.shape
    ensemble = bricks * part
    gates = obs_ref.shape[1]
    tail = taper_ref.shape[1]
    cap = index_ref.shape[0] // bricks
    block = (out_rows - tail) // cap
    held_rows = cap * gates
    at_m = lax.axis_index("mem")
    at_b = lax.axis_index("brick")
    mesh_ids = pl.DeviceIdType.MESH

    barrier = pltpu.get_barrier_semaphore()
    for d in range(1, bricks):
        pl.semaphore_signal(
            barrier, inc=1, device_id=(at_m, lax.rem(at_b + d, bricks)), device_id_type=mesh_ids
        )
    for e in range(1, mem_count):
        pl.semaphore_signal(
            barrier, inc=1, device_id=(lax.rem(at_m + e, mem_count), at_b), device_id_type=mesh_ids
        )
    pl.semaphore_wait(barrier, bricks + mem_count - 2)

    def along_brick(d, source, target, send_sem, recv_sem):
        there = lax.rem(at_b + d, bricks)
        return pltpu.make_async_remote_copy(
            src_ref=source.at[there],
            dst_ref=target.at[at_b],
            send_sem=send_sem.at[d],
            recv_sem=recv_sem.at[d],
            device_id=(at_m, there),
            device_id_type=mesh_ids,
        )

    piece = soundings // PIECES

    def send_pair(d, h):
        there = lax.rem(at_b + d, bricks)
        return pltpu.make_async_remote_copy(
            src_ref=pair_ref.at[there, pl.ds(h * piece, piece)],
            dst_ref=data.at[at_b, pl.ds(h * piece, piece)],
            send_sem=p_send.at[h * bricks + d],
            recv_sem=p_recv.at[h * bricks + d],
            device_id=(at_m, there),
            device_id_type=mesh_ids,
        )

    def send_anomaly(d):
        return along_brick(d, stage_a, landed_a, a_send, a_recv)

    def send_gain(d):
        return along_brick(d, stage_g, landed_g, g_send, g_recv)

    def to_member(d, e):
        source = lax.rem(at_b - d + bricks, bricks)
        there = lax.rem(at_m + e, mem_count)
        return pltpu.make_async_remote_copy(
            src_ref=spread.at[source, there],
            dst_ref=out_ref.at[at_m, source],
            send_sem=m_send.at[d * mem_count + e],
            recv_sem=m_recv.at[d * mem_count + e],
            device_id=(there, at_b),
            device_id_type=mesh_ids,
        )

    def each_peer(step):
        def turn(d, carry):
            step(d)
            return carry

        lax.fori_loop(1, bricks, turn, 0)

    for h in range(PIECES):
        each_peer(lambda d: send_pair(d, h).start())
    data[at_b] = pair_ref[at_b]

    row = lax.broadcasted_iota(jnp.int32, (gates, gates), 0)
    column = lax.broadcasted_iota(jnp.int32, (gates, gates), 1)

    def prepare(s, carry):
        turned = data[:, s].astype(jnp.float32).reshape(ensemble, lanes).T
        pred = turned[:gates]
        pert = turned[gates : 2 * gates]
        std = std_ref[s]
        anomaly = pred - jnp.sum(pred, axis=1, keepdims=True) / ensemble
        misf[s] = obs_ref[s] + std * pert - pred
        anom[s] = anomaly
        total = lax.dot_general(
            anomaly,
            anomaly,
            (((1,), (1,)), ((), ())),
            precision=HIGH,
            preferred_element_type=jnp.float32,
        ) / (ensemble - 1.0)
        cov[s] = total + jnp.where(row == column, std * std, 0.0)
        return carry

    for h in range(PIECES):
        each_peer(lambda d: send_pair(d, h).wait())
        lax.fori_loop(h * piece, (h + 1) * piece, prepare, 0, unroll=4)

    def pack(values, ref, place, there):
        for r in range(0, cap, 2):
            first = values[index_ref[there * cap + r]]
            second = values[index_ref[there * cap + r + 1]]
            both = jnp.concatenate([first, second], axis=0).astype(jnp.bfloat16)
            ref[place, pl.ds(r * gates, 2 * gates), :] = both

    def post_anomaly(d):
        there = lax.rem(at_b + d, bricks)
        pack(anom, stage_a, there, there)
        stage_a[there, pl.ds(held_rows, tail), :] = taper_ref[there]
        send_anomaly(d).start()

    each_peer(post_anomaly)
    pack(anom, landed_a, at_b, at_b)
    landed_a[at_b, pl.ds(held_rows, tail), :] = taper_ref[at_b]

    for i in range(gates):
        work[i] = cov[:, i, :].T

    place = lax.broadcasted_iota(jnp.int32, (gates, soundings), 0)

    def sweep(k, carry):
        scale = 1.0 / work[k, pl.ds(k, 1), :]
        pivot = work[k]
        scaled = jnp.where(place == k, scale, pivot * scale)
        kept = jnp.where(place == k, 0.0, 1.0)
        for i in range(gates):
            coef = work[i, pl.ds(k, 1), :]
            work[i] = work[i] * kept - coef * scaled
        work[k] = scaled
        return carry

    lax.fori_loop(0, gates, sweep, 0)

    for i in range(gates):
        inv[:, i, :] = work[i].T

    def finish(s, carry):
        misf[s] = lax.dot_general(
            inv[s],
            misf[s],
            (((1,), (0,)), ((), ())),
            precision=HIGH,
            preferred_element_type=jnp.float32,
        ) / (ensemble - 1.0)
        return carry

    lax.fori_loop(0, soundings, finish, 0, unroll=4)

    def post_gain(d):
        there = lax.rem(at_b + d, bricks)
        pack(misf, stage_g, there, there)
        send_gain(d).start()

    each_peer(post_gain)
    pack(misf, landed_g, at_b, at_b)

    first = lax.broadcasted_iota(jnp.int32, (2 * gates, ensemble), 0) < gates

    def weigh(d):
        source = lax.rem(at_b - d + bricks, bricks)
        for r in range(0, cap, 2):
            gains = landed_g[source, pl.ds(r * gates, 2 * gates), :].astype(jnp.float32)
            anomalies = landed_a[source, pl.ds(r * gates, 2 * gates), :].astype(jnp.float32)
            sides = jnp.concatenate(
                [jnp.where(first, anomalies, 0.0), jnp.where(first, 0.0, anomalies)], axis=1
            )
            weight = jnp.dot(
                gains.T.astype(jnp.bfloat16),
                sides.astype(jnp.bfloat16),
                preferred_element_type=jnp.float32,
            ).astype(jnp.bfloat16)
            for h in range(2):
                for m in range(mem_count):
                    spread[source, m, pl.ds((r + h) * block, block), :] = weight[
                        m * block : (m + 1) * block, h * ensemble : (h + 1) * ensemble
                    ]
        tapers = landed_a[source, pl.ds(held_rows, tail), :]
        for m in range(mem_count):
            spread[source, m, pl.ds(cap * block, tail), :] = tapers
        for e in range(1, mem_count):
            to_member(d, e).start()
        out_ref[at_m, source] = spread[source, at_m]

    weigh(0)

    def take(d):
        send_anomaly(d).wait_recv()
        send_gain(d).wait_recv()
        weigh(d)

    each_peer(take)

    def sent(d):
        send_anomaly(d).wait_send()
        send_gain(d).wait_send()

    each_peer(sent)

    def settle(d, carry):
        for e in range(1, mem_count):
            to_member(d, e).wait()
        return carry

    lax.fori_loop(0, bricks, settle, 0)


def update_kernel(
    count_ref, slot_ref, tile_ref, recv_ref, model_ref, members_ref, out_ref, tapers
):
    foot = tile_ref.shape[0]
    block = members_ref.shape[0]
    cap = slot_ref.shape[0] // recv_ref.shape[0]
    total = count_ref[0]
    out_ref[...] = members_ref[...]
    tapers[...] = recv_ref[:, cap * block : cap * (block + foot), :].astype(jnp.float32)

    def turn(step, carry):
        results = []
        for u in range(GROUP):
            at = step * GROUP + u
            owner = slot_ref[at] // cap
            rank = slot_ref[at] % cap
            weight = recv_ref[owner, pl.ds(pl.multiple_of(rank * block, block), block), :]
            used = at < total
            starts = [pl.multiple_of(tile_ref[c, at] * 128, 128) for c in range(foot)]
            for c, start in enumerate(starts):
                taper = tapers[owner, pl.ds(rank * foot + c, 1), :]
                part = jnp.dot(
                    weight, model_ref[:, pl.ds(start, 128)], preferred_element_type=jnp.float32
                )
                scaled = part * taper
                results.append((start, jnp.where(used, scaled, 0.0)))
        for start, scaled in results:
            out_ref[:, pl.ds(start, 128)] += scaled
        return carry

    lax.fori_loop(0, (total + GROUP - 1) // GROUP, turn, 0)


def body(
    members, predicted, perturbation, observed, noise_std, taper_weights, foot_brick, foot_tiles
):
    mem_count = lax.axis_size("mem")
    brick_count = lax.axis_size("brick")
    part, gates, wide = predicted.shape
    ensemble = part * brick_count
    local = wide // brick_count
    block = ensemble // mem_count
    foot = foot_tiles.shape[1]
    foot_length = taper_weights.shape[1]
    devices = mem_count * brick_count
    cap = max(2, 2 * local // brick_count)
    slots = devices * cap
    vmem = pltpu.CompilerParams(vmem_limit_bytes=48 * 1024 * 1024)
    in_vmem = pl.BlockSpec(memory_space=pltpu.VMEM)
    in_smem = pl.BlockSpec(memory_space=pltpu.SMEM)

    model_all = lax.all_gather(members.astype(jnp.bfloat16), "mem", axis=0, tiled=True)

    pair = jnp.concatenate([predicted, perturbation], axis=1).astype(jnp.bfloat16)
    pair = jnp.transpose(pair, (2, 0, 1))
    pair = jnp.pad(pair, ((0, 0), (0, 0), (0, 128 - 2 * gates)))
    pair = pair.reshape(brick_count, local, part, 128)
    destination = foot_brick[:, 0]
    order = jnp.arange(local)
    before = order[None, :] < order[:, None]
    rank = jnp.sum(
        ((destination[:, None] == destination[None, :]) & before).astype(jnp.int32), axis=1
    )
    slot_of = destination * cap + rank
    hot = slot_of[None, :] == jnp.arange(brick_count * cap, dtype=jnp.int32)[:, None]
    index = jnp.sum(jnp.where(hot, order[None, :], 0), axis=1)
    numbers = jnp.concatenate([foot_tiles, jnp.ones((local, 1), jnp.int32)], axis=1)
    numbers = jnp.pad(numbers.astype(jnp.bfloat16), ((0, 0), (0, 127 - foot)))
    extra = jnp.concatenate([taper_weights, numbers], axis=1)
    extra = jnp.dot(hot.astype(jnp.bfloat16), extra, preferred_element_type=jnp.float32)
    extra = extra.astype(jnp.bfloat16)
    taper_slots = extra[:, :foot_length].reshape(brick_count, cap * foot, 128)
    number_slots = extra[:, foot_length:].reshape(brick_count, cap, 128)
    tail = -(-cap * (foot + 1) // 16) * 16
    taper_slots = jnp.concatenate([taper_slots, number_slots], axis=1)
    taper_slots = jnp.pad(taper_slots, ((0, 0), (0, tail - cap * (foot + 1)), (0, 0)))

    out_rows = cap * block + tail
    recv = pl.pallas_call(
        owner_kernel,
        out_shape=jax.ShapeDtypeStruct((mem_count, brick_count, out_rows, 128), jnp.bfloat16),
        in_specs=[in_smem] + [in_vmem] * 4,
        out_specs=in_vmem,
        scratch_shapes=[
            pltpu.VMEM(pair.shape, jnp.bfloat16),
            pltpu.VMEM((local, gates, ensemble), jnp.float32),
            pltpu.VMEM((local, gates, ensemble), jnp.float32),
            pltpu.VMEM((local, gates, gates), jnp.float32),
            pltpu.VMEM((gates, gates, local), jnp.float32),
            pltpu.VMEM((local, gates, gates), jnp.float32),
            pltpu.VMEM((brick_count, cap * gates + tail, 128), jnp.bfloat16),
            pltpu.VMEM((brick_count, cap * gates, 128), jnp.bfloat16),
            pltpu.VMEM((brick_count, cap * gates + tail, 128), jnp.bfloat16),
            pltpu.VMEM((brick_count, cap * gates, 128), jnp.bfloat16),
            pltpu.VMEM((brick_count, mem_count, out_rows, 128), jnp.bfloat16),
        ]
        + [pltpu.SemaphoreType.DMA((brick_count * PIECES,))] * 2
        + [pltpu.SemaphoreType.DMA((brick_count,))] * 4
        + [pltpu.SemaphoreType.DMA((brick_count * mem_count,))] * 2,
        compiler_params=pltpu.CompilerParams(
            vmem_limit_bytes=48 * 1024 * 1024, collective_id=0, has_side_effects=True
        ),
        cost_estimate=pl.CostEstimate(
            flops=20_000_000_000, bytes_accessed=200_000_000, transcendentals=0
        ),
    )(
        index,
        pair,
        jnp.transpose(observed)[:, :, None],
        jnp.transpose(noise_std)[:, :, None],
        taper_slots,
    ).reshape(devices, out_rows, 128)

    numbers = recv[:, cap * (block + foot) : cap * (block + foot + 1), : foot + 1]
    numbers = numbers.astype(jnp.float32).astype(jnp.int32).reshape(slots, foot + 1)
    filled = numbers[:, foot] == 1
    spots = jnp.arange(slots)
    position = jnp.sum((filled[None, :] & (spots[None, :] < spots[:, None])).astype(jnp.int32), axis=1)
    listed = filled[None, :] & (position[None, :] == spots[:, None])
    slot_list = jnp.sum(jnp.where(listed, spots[None, :], 0), axis=1)
    tile_list = jnp.sum(
        jnp.where(listed[None], jnp.transpose(numbers[:, :foot])[:, None, :], 0), axis=2
    )
    count = jnp.sum(filled.astype(jnp.int32)).reshape(1)

    return pl.pallas_call(
        update_kernel,
        out_shape=jax.ShapeDtypeStruct(members.shape, members.dtype),
        in_specs=[in_smem] * 3 + [in_vmem] * 3,
        out_specs=in_vmem,
        scratch_shapes=[pltpu.VMEM((devices, cap * foot, 128), jnp.float32)],
        compiler_params=vmem,
        cost_estimate=pl.CostEstimate(flops=600_000_000, bytes_accessed=10_000_000, transcendentals=0),
    )(count, slot_list, tile_list, recv, model_all, members)


def solution(mesh):
    in_specs = (
        P("mem", "brick"),
        P("brick", None, "mem"),
        P("brick", None, "mem"),
        P(None, ("mem", "brick")),
        P(None, ("mem", "brick")),
        P(("mem", "brick"), None),
        P(("mem", "brick"), None),
        P(("mem", "brick"), None),
    )
    out_specs = P("mem", "brick")
    return jax.shard_map(body, mesh=mesh, in_specs=in_specs, out_specs=out_specs, check_vma=False)
```

```python
import jax
import jax.numpy as jnp
from jax import lax
from jax.experimental import pallas as pl
from jax.experimental.pallas import tpu as pltpu
from jax.sharding import PartitionSpec as P

GROUP = 8
PIECES = 4
HIGH = lax.Precision.HIGHEST


def owner_kernel(
    index_ref,
    pair_ref,
    obs_ref,
    std_ref,
    taper_ref,
    out_ref,
    data,
    anom,
    misf,
    cov,
    work,
    inv,
    stage_a,
    stage_g,
    landed_a,
    landed_g,
    spread,
    p_send,
    p_recv,
    a_send,
    a_recv,
    g_send,
    g_recv,
    m_send,
    m_recv,
):
    mem_count, bricks, out_rows, _ = out_ref.shape
    _, soundings, part, lanes = pair_ref.shape
    ensemble = bricks * part
    gates = obs_ref.shape[1]
    tail = taper_ref.shape[1]
    cap = index_ref.shape[0] // bricks
    block = (out_rows - tail) // cap
    held_rows = cap * gates
    at_m = lax.axis_index("mem")
    at_b = lax.axis_index("brick")
    mesh_ids = pl.DeviceIdType.MESH

    barrier = pltpu.get_barrier_semaphore()
    for d in range(1, bricks):
        pl.semaphore_signal(
            barrier, inc=1, device_id=(at_m, lax.rem(at_b + d, bricks)), device_id_type=mesh_ids
        )
    for e in range(1, mem_count):
        pl.semaphore_signal(
            barrier, inc=1, device_id=(lax.rem(at_m + e, mem_count), at_b), device_id_type=mesh_ids
        )
    pl.semaphore_wait(barrier, bricks + mem_count - 2)

    def along_brick(d, source, target, send_sem, recv_sem):
        there = lax.rem(at_b + d, bricks)
        return pltpu.make_async_remote_copy(
            src_ref=source.at[there],
            dst_ref=target.at[at_b],
            send_sem=send_sem.at[d],
            recv_sem=recv_sem.at[d],
            device_id=(at_m, there),
            device_id_type=mesh_ids,
        )

    piece = soundings // PIECES

    def send_pair(d, h):
        there = lax.rem(at_b + d, bricks)
        return pltpu.make_async_remote_copy(
            src_ref=pair_ref.at[there, pl.ds(h * piece, piece)],
            dst_ref=data.at[at_b, pl.ds(h * piece, piece)],
            send_sem=p_send.at[h * bricks + d],
            recv_sem=p_recv.at[h * bricks + d],
            device_id=(at_m, there),
            device_id_type=mesh_ids,
        )

    def send_anomaly(d):
        return along_brick(d, stage_a, landed_a, a_send, a_recv)

    def send_gain(d):
        return along_brick(d, stage_g, landed_g, g_send, g_recv)

    def to_member(d, e):
        source = lax.rem(at_b - d + bricks, bricks)
        there = lax.rem(at_m + e, mem_count)
        return pltpu.make_async_remote_copy(
            src_ref=spread.at[source, there],
            dst_ref=out_ref.at[at_m, source],
            send_sem=m_send.at[d * mem_count + e],
            recv_sem=m_recv.at[d * mem_count + e],
            device_id=(there, at_b),
            device_id_type=mesh_ids,
        )

    def each_peer(step):
        def turn(d, carry):
            step(d)
            return carry

        lax.fori_loop(1, bricks, turn, 0)

    for h in range(PIECES):
        each_peer(lambda d: send_pair(d, h).start())
    data[at_b] = pair_ref[at_b]

    row = lax.broadcasted_iota(jnp.int32, (gates, gates), 0)
    column = lax.broadcasted_iota(jnp.int32, (gates, gates), 1)

    def prepare(s, carry):
        turned = data[:, s].astype(jnp.float32).reshape(ensemble, lanes).T
        pred = turned[:gates]
        pert = turned[gates : 2 * gates]
        std = std_ref[s]
        anomaly = pred - jnp.sum(pred, axis=1, keepdims=True) / ensemble
        misf[s] = obs_ref[s] + std * pert - pred
        anom[s] = anomaly
        total = lax.dot_general(
            anomaly,
            anomaly,
            (((1,), (1,)), ((), ())),
            precision=HIGH,
            preferred_element_type=jnp.float32,
        ) / (ensemble - 1.0)
        cov[s] = total + jnp.where(row == column, std * std, 0.0)
        return carry

    for h in range(PIECES):
        each_peer(lambda d: send_pair(d, h).wait())
        lax.fori_loop(h * piece, (h + 1) * piece, prepare, 0, unroll=4)

    def pack(values, ref, place, there):
        for r in range(0, cap, 2):
            first = values[index_ref[there * cap + r]]
            second = values[index_ref[there * cap + r + 1]]
            both = jnp.concatenate([first, second], axis=0).astype(jnp.bfloat16)
            ref[place, pl.ds(r * gates, 2 * gates), :] = both

    def post_anomaly(d):
        there = lax.rem(at_b + d, bricks)
        pack(anom, stage_a, there, there)
        stage_a[there, pl.ds(held_rows, tail), :] = taper_ref[there]
        send_anomaly(d).start()

    each_peer(post_anomaly)
    pack(anom, landed_a, at_b, at_b)
    landed_a[at_b, pl.ds(held_rows, tail), :] = taper_ref[at_b]

    for i in range(gates):
        work[i] = cov[:, i, :].T

    place = lax.broadcasted_iota(jnp.int32, (gates, soundings), 0)

    def sweep(k, carry):
        scale = 1.0 / work[k, pl.ds(k, 1), :]
        pivot = work[k]
        scaled = jnp.where(place == k, scale, pivot * scale)
        kept = jnp.where(place == k, 0.0, 1.0)
        for i in range(gates):
            coef = work[i, pl.ds(k, 1), :]
            work[i] = work[i] * kept - coef * scaled
        work[k] = scaled
        return carry

    lax.fori_loop(0, gates, sweep, 0)

    for i in range(gates):
        inv[:, i, :] = work[i].T

    def finish(s, carry):
        misf[s] = lax.dot_general(
            inv[s],
            misf[s],
            (((1,), (0,)), ((), ())),
            precision=HIGH,
            preferred_element_type=jnp.float32,
        ) / (ensemble - 1.0)
        return carry

    lax.fori_loop(0, soundings, finish, 0, unroll=4)

    def post_gain(d):
        there = lax.rem(at_b + d, bricks)
        pack(misf, stage_g, there, there)
        send_gain(d).start()

    each_peer(post_gain)
    pack(misf, landed_g, at_b, at_b)

    first = lax.broadcasted_iota(jnp.int32, (2 * gates, ensemble), 0) < gates

    def weigh(d):
        source = lax.rem(at_b - d + bricks, bricks)
        for r in range(0, cap, 2):
            gains = landed_g[source, pl.ds(r * gates, 2 * gates), :].astype(jnp.float32)
            anomalies = landed_a[source, pl.ds(r * gates, 2 * gates), :].astype(jnp.float32)
            sides = jnp.concatenate(
                [jnp.where(first, anomalies, 0.0), jnp.where(first, 0.0, anomalies)], axis=1
            )
            weight = jnp.dot(
                gains.T.astype(jnp.bfloat16),
                sides.astype(jnp.bfloat16),
                preferred_element_type=jnp.float32,
            ).astype(jnp.bfloat16)
            for h in range(2):
                for m in range(mem_count):
                    spread[source, m, pl.ds((r + h) * block, block), :] = weight[
                        m * block : (m + 1) * block, h * ensemble : (h + 1) * ensemble
                    ]
        tapers = landed_a[source, pl.ds(held_rows, tail), :]
        for m in range(mem_count):
            spread[source, m, pl.ds(cap * block, tail), :] = tapers
        for e in range(1, mem_count):
            to_member(d, e).start()
        out_ref[at_m, source] = spread[source, at_m]

    weigh(0)

    def take(d):
        send_anomaly(d).wait_recv()
        send_gain(d).wait_recv()
        weigh(d)

    each_peer(take)

    def sent(d):
        send_anomaly(d).wait_send()
        send_gain(d).wait_send()

    each_peer(sent)

    def settle(d, carry):
        for e in range(1, mem_count):
            to_member(d, e).wait()
        return carry

    lax.fori_loop(0, bricks, settle, 0)


def update_kernel(
    count_ref, slot_ref, tile_ref, recv_ref, model_ref, members_ref, out_ref, tapers
):
    foot = tile_ref.shape[0]
    block = members_ref.shape[0]
    cap = slot_ref.shape[0] // recv_ref.shape[0]
    total = count_ref[0]
    out_ref[...] = members_ref[...]
    tapers[...] = recv_ref[:, cap * block : cap * (block + foot), :].astype(jnp.float32)

    def turn(step, carry):
        results = []
        for u in range(GROUP):
            at = step * GROUP + u
            owner = slot_ref[at] // cap
            rank = slot_ref[at] % cap
            weight = recv_ref[owner, pl.ds(pl.multiple_of(rank * block, block), block), :]
            used = at < total
            starts = [pl.multiple_of(tile_ref[c, at] * 128, 128) for c in range(foot)]
            for c, start in enumerate(starts):
                taper = tapers[owner, pl.ds(rank * foot + c, 1), :]
                part = jnp.dot(
                    weight, model_ref[:, pl.ds(start, 128)], preferred_element_type=jnp.float32
                )
                scaled = part * taper
                results.append((start, jnp.where(used, scaled, 0.0)))
        for start, scaled in results:
            out_ref[:, pl.ds(start, 128)] += scaled
        return carry

    lax.fori_loop(0, (total + GROUP - 1) // GROUP, turn, 0)


def body(
    members, predicted, perturbation, observed, noise_std, taper_weights, foot_brick, foot_tiles
):
    mem_count = lax.axis_size("mem")
    brick_count = lax.axis_size("brick")
    part, gates, wide = predicted.shape
    ensemble = part * brick_count
    local = wide // brick_count
    block = ensemble // mem_count
    foot = foot_tiles.shape[1]
    foot_length = taper_weights.shape[1]
    devices = mem_count * brick_count
    cap = max(2, 2 * local // brick_count)
    slots = devices * cap
    vmem = pltpu.CompilerParams(vmem_limit_bytes=24 * 1024 * 1024)
    in_vmem = pl.BlockSpec(memory_space=pltpu.VMEM)
    in_smem = pl.BlockSpec(memory_space=pltpu.SMEM)

    model_all = lax.all_gather(members.astype(jnp.bfloat16), "mem", axis=0, tiled=True)

    pair = jnp.concatenate([predicted, perturbation], axis=1).astype(jnp.bfloat16)
    pair = jnp.transpose(pair, (2, 0, 1))
    pair = jnp.pad(pair, ((0, 0), (0, 0), (0, 128 - 2 * gates)))
    pair = pair.reshape(brick_count, local, part, 128)
    destination = foot_brick[:, 0]
    order = jnp.arange(local)
    before = order[None, :] < order[:, None]
    rank = jnp.sum(
        ((destination[:, None] == destination[None, :]) & before).astype(jnp.int32), axis=1
    )
    slot_of = destination * cap + rank
    hot = slot_of[None, :] == jnp.arange(brick_count * cap, dtype=jnp.int32)[:, None]
    index = jnp.sum(jnp.where(hot, order[None, :], 0), axis=1)
    numbers = jnp.concatenate([foot_tiles, jnp.ones((local, 1), jnp.int32)], axis=1)
    numbers = jnp.pad(numbers.astype(jnp.bfloat16), ((0, 0), (0, 127 - foot)))
    extra = jnp.concatenate([taper_weights, numbers], axis=1)
    extra = jnp.dot(hot.astype(jnp.bfloat16), extra, preferred_element_type=jnp.float32)
    extra = extra.astype(jnp.bfloat16)
    taper_slots = extra[:, :foot_length].reshape(brick_count, cap * foot, 128)
    number_slots = extra[:, foot_length:].reshape(brick_count, cap, 128)
    tail = -(-cap * (foot + 1) // 16) * 16
    taper_slots = jnp.concatenate([taper_slots, number_slots], axis=1)
    taper_slots = jnp.pad(taper_slots, ((0, 0), (0, tail - cap * (foot + 1)), (0, 0)))

    out_rows = cap * block + tail
    recv = pl.pallas_call(
        owner_kernel,
        out_shape=jax.ShapeDtypeStruct((mem_count, brick_count, out_rows, 128), jnp.bfloat16),
        in_specs=[in_smem] + [in_vmem] * 4,
        out_specs=in_vmem,
        scratch_shapes=[
            pltpu.VMEM(pair.shape, jnp.bfloat16),
            pltpu.VMEM((local, gates, ensemble), jnp.float32),
            pltpu.VMEM((local, gates, ensemble), jnp.float32),
            pltpu.VMEM((local, gates, gates), jnp.float32),
            pltpu.VMEM((gates, gates, local), jnp.float32),
            pltpu.VMEM((local, gates, gates), jnp.float32),
            pltpu.VMEM((brick_count, cap * gates + tail, 128), jnp.bfloat16),
            pltpu.VMEM((brick_count, cap * gates, 128), jnp.bfloat16),
            pltpu.VMEM((brick_count, cap * gates + tail, 128), jnp.bfloat16),
            pltpu.VMEM((brick_count, cap * gates, 128), jnp.bfloat16),
            pltpu.VMEM((brick_count, mem_count, out_rows, 128), jnp.bfloat16),
        ]
        + [pltpu.SemaphoreType.DMA((brick_count * PIECES,))] * 2
        + [pltpu.SemaphoreType.DMA((brick_count,))] * 4
        + [pltpu.SemaphoreType.DMA((brick_count * mem_count,))] * 2,
        compiler_params=pltpu.CompilerParams(
            vmem_limit_bytes=24 * 1024 * 1024, collective_id=0, has_side_effects=True
        ),
        cost_estimate=pl.CostEstimate(
            flops=20_000_000_000, bytes_accessed=200_000_000, transcendentals=0
        ),
    )(
        index,
        pair,
        jnp.transpose(observed)[:, :, None],
        jnp.transpose(noise_std)[:, :, None],
        taper_slots,
    ).reshape(devices, out_rows, 128)

    numbers = recv[:, cap * (block + foot) : cap * (block + foot + 1), : foot + 1]
    numbers = numbers.astype(jnp.float32).astype(jnp.int32).reshape(slots, foot + 1)
    filled = numbers[:, foot] == 1
    spots = jnp.arange(slots)
    position = jnp.sum((filled[None, :] & (spots[None, :] < spots[:, None])).astype(jnp.int32), axis=1)
    listed = filled[None, :] & (position[None, :] == spots[:, None])
    slot_list = jnp.sum(jnp.where(listed, spots[None, :], 0), axis=1)
    tile_list = jnp.sum(
        jnp.where(listed[None], jnp.transpose(numbers[:, :foot])[:, None, :], 0), axis=2
    )
    count = jnp.sum(filled.astype(jnp.int32)).reshape(1)

    return pl.pallas_call(
        update_kernel,
        out_shape=jax.ShapeDtypeStruct(members.shape, members.dtype),
        in_specs=[in_smem] * 3 + [in_vmem] * 3,
        out_specs=in_vmem,
        scratch_shapes=[pltpu.VMEM((devices, cap * foot, 128), jnp.float32)],
        compiler_params=vmem,
        cost_estimate=pl.CostEstimate(flops=600_000_000, bytes_accessed=10_000_000, transcendentals=0),
    )(count, slot_list, tile_list, recv, model_all, members)


def solution(mesh):
    in_specs = (
        P("mem", "brick"),
        P("brick", None, "mem"),
        P("brick", None, "mem"),
        P(None, ("mem", "brick")),
        P(None, ("mem", "brick")),
        P(("mem", "brick"), None),
        P(("mem", "brick"), None),
        P(("mem", "brick"), None),
    )
    out_specs = P("mem", "brick")
    return jax.shard_map(body, mesh=mesh, in_specs=in_specs, out_specs=out_specs, check_vma=False)
```

```python
import jax
import jax.numpy as jnp
from jax import lax
from jax.experimental import pallas as pl
from jax.experimental.pallas import tpu as pltpu
from jax.sharding import PartitionSpec as P

GROUP = 16
PIECES = 4
HIGH = lax.Precision.HIGHEST


def owner_kernel(
    index_ref,
    pair_ref,
    obs_ref,
    std_ref,
    taper_ref,
    out_ref,
    data,
    anom,
    misf,
    cov,
    work,
    inv,
    stage_a,
    stage_g,
    landed_a,
    landed_g,
    spread,
    p_send,
    p_recv,
    a_send,
    a_recv,
    g_send,
    g_recv,
    m_send,
    m_recv,
):
    mem_count, bricks, out_rows, _ = out_ref.shape
    _, soundings, part, lanes = pair_ref.shape
    ensemble = bricks * part
    gates = obs_ref.shape[1]
    tail = taper_ref.shape[1]
    cap = index_ref.shape[0] // bricks
    block = (out_rows - tail) // cap
    held_rows = cap * gates
    at_m = lax.axis_index("mem")
    at_b = lax.axis_index("brick")
    mesh_ids = pl.DeviceIdType.MESH

    barrier = pltpu.get_barrier_semaphore()
    for d in range(1, bricks):
        pl.semaphore_signal(
            barrier, inc=1, device_id=(at_m, lax.rem(at_b + d, bricks)), device_id_type=mesh_ids
        )
    for e in range(1, mem_count):
        pl.semaphore_signal(
            barrier, inc=1, device_id=(lax.rem(at_m + e, mem_count), at_b), device_id_type=mesh_ids
        )
    pl.semaphore_wait(barrier, bricks + mem_count - 2)

    def along_brick(d, source, target, send_sem, recv_sem):
        there = lax.rem(at_b + d, bricks)
        return pltpu.make_async_remote_copy(
            src_ref=source.at[there],
            dst_ref=target.at[at_b],
            send_sem=send_sem.at[d],
            recv_sem=recv_sem.at[d],
            device_id=(at_m, there),
            device_id_type=mesh_ids,
        )

    piece = soundings // PIECES

    def send_pair(d, h):
        there = lax.rem(at_b + d, bricks)
        return pltpu.make_async_remote_copy(
            src_ref=pair_ref.at[there, pl.ds(h * piece, piece)],
            dst_ref=data.at[at_b, pl.ds(h * piece, piece)],
            send_sem=p_send.at[h * bricks + d],
            recv_sem=p_recv.at[h * bricks + d],
            device_id=(at_m, there),
            device_id_type=mesh_ids,
        )

    def send_anomaly(d):
        return along_brick(d, stage_a, landed_a, a_send, a_recv)

    def send_gain(d):
        return along_brick(d, stage_g, landed_g, g_send, g_recv)

    def to_member(d, e):
        source = lax.rem(at_b - d + bricks, bricks)
        there = lax.rem(at_m + e, mem_count)
        return pltpu.make_async_remote_copy(
            src_ref=spread.at[source, there],
            dst_ref=out_ref.at[at_m, source],
            send_sem=m_send.at[d * mem_count + e],
            recv_sem=m_recv.at[d * mem_count + e],
            device_id=(there, at_b),
            device_id_type=mesh_ids,
        )

    def each_peer(step):
        def turn(d, carry):
            step(d)
            return carry

        lax.fori_loop(1, bricks, turn, 0)

    for h in range(PIECES):
        each_peer(lambda d: send_pair(d, h).start())
    data[at_b] = pair_ref[at_b]

    row = lax.broadcasted_iota(jnp.int32, (gates, gates), 0)
    column = lax.broadcasted_iota(jnp.int32, (gates, gates), 1)

    def prepare(s, carry):
        turned = data[:, s].astype(jnp.float32).reshape(ensemble, lanes).T
        pred = turned[:gates]
        pert = turned[gates : 2 * gates]
        std = std_ref[s]
        anomaly = pred - jnp.sum(pred, axis=1, keepdims=True) / ensemble
        misf[s] = obs_ref[s] + std * pert - pred
        anom[s] = anomaly
        total = lax.dot_general(
            anomaly,
            anomaly,
            (((1,), (1,)), ((), ())),
            precision=HIGH,
            preferred_element_type=jnp.float32,
        ) / (ensemble - 1.0)
        cov[s] = total + jnp.where(row == column, std * std, 0.0)
        return carry

    for h in range(PIECES):
        each_peer(lambda d: send_pair(d, h).wait())
        lax.fori_loop(h * piece, (h + 1) * piece, prepare, 0, unroll=4)

    def pack(values, ref, place, there):
        for r in range(0, cap, 2):
            first = values[index_ref[there * cap + r]]
            second = values[index_ref[there * cap + r + 1]]
            both = jnp.concatenate([first, second], axis=0).astype(jnp.bfloat16)
            ref[place, pl.ds(r * gates, 2 * gates), :] = both

    def post_anomaly(d):
        there = lax.rem(at_b + d, bricks)
        pack(anom, stage_a, there, there)
        stage_a[there, pl.ds(held_rows, tail), :] = taper_ref[there]
        send_anomaly(d).start()

    each_peer(post_anomaly)
    pack(anom, landed_a, at_b, at_b)
    landed_a[at_b, pl.ds(held_rows, tail), :] = taper_ref[at_b]

    for i in range(gates):
        work[i] = cov[:, i, :].T

    place = lax.broadcasted_iota(jnp.int32, (gates, soundings), 0)

    def sweep(k, carry):
        scale = 1.0 / work[k, pl.ds(k, 1), :]
        pivot = work[k]
        scaled = jnp.where(place == k, scale, pivot * scale)
        kept = jnp.where(place == k, 0.0, 1.0)
        for i in range(gates):
            coef = work[i, pl.ds(k, 1), :]
            work[i] = work[i] * kept - coef * scaled
        work[k] = scaled
        return carry

    lax.fori_loop(0, gates, sweep, 0)

    for i in range(gates):
        inv[:, i, :] = work[i].T

    def finish(s, carry):
        misf[s] = lax.dot_general(
            inv[s],
            misf[s],
            (((1,), (0,)), ((), ())),
            precision=HIGH,
            preferred_element_type=jnp.float32,
        ) / (ensemble - 1.0)
        return carry

    lax.fori_loop(0, soundings, finish, 0, unroll=4)

    def post_gain(d):
        there = lax.rem(at_b + d, bricks)
        pack(misf, stage_g, there, there)
        send_gain(d).start()

    each_peer(post_gain)
    pack(misf, landed_g, at_b, at_b)

    first = lax.broadcasted_iota(jnp.int32, (2 * gates, ensemble), 0) < gates

    def weigh(d):
        source = lax.rem(at_b - d + bricks, bricks)
        for r in range(0, cap, 2):
            gains = landed_g[source, pl.ds(r * gates, 2 * gates), :].astype(jnp.float32)
            anomalies = landed_a[source, pl.ds(r * gates, 2 * gates), :].astype(jnp.float32)
            sides = jnp.concatenate(
                [jnp.where(first, anomalies, 0.0), jnp.where(first, 0.0, anomalies)], axis=1
            )
            weight = jnp.dot(
                gains.T.astype(jnp.bfloat16),
                sides.astype(jnp.bfloat16),
                preferred_element_type=jnp.float32,
            ).astype(jnp.bfloat16)
            for h in range(2):
                for m in range(mem_count):
                    spread[source, m, pl.ds((r + h) * block, block), :] = weight[
                        m * block : (m + 1) * block, h * ensemble : (h + 1) * ensemble
                    ]
        tapers = landed_a[source, pl.ds(held_rows, tail), :]
        for m in range(mem_count):
            spread[source, m, pl.ds(cap * block, tail), :] = tapers
        for e in range(1, mem_count):
            to_member(d, e).start()
        out_ref[at_m, source] = spread[source, at_m]

    weigh(0)

    def take(d):
        send_anomaly(d).wait_recv()
        send_gain(d).wait_recv()
        weigh(d)

    each_peer(take)

    def sent(d):
        send_anomaly(d).wait_send()
        send_gain(d).wait_send()

    each_peer(sent)

    def settle(d, carry):
        for e in range(1, mem_count):
            to_member(d, e).wait()
        return carry

    lax.fori_loop(0, bricks, settle, 0)


def update_kernel(
    count_ref, slot_ref, tile_ref, recv_ref, model_ref, members_ref, out_ref, tapers
):
    foot = tile_ref.shape[0]
    block = members_ref.shape[0]
    cap = slot_ref.shape[0] // recv_ref.shape[0]
    total = count_ref[0]
    out_ref[...] = members_ref[...]
    tapers[...] = recv_ref[:, cap * block : cap * (block + foot), :].astype(jnp.float32)

    def turn(step, carry):
        results = []
        for u in range(GROUP):
            at = step * GROUP + u
            owner = slot_ref[at] // cap
            rank = slot_ref[at] % cap
            weight = recv_ref[owner, pl.ds(pl.multiple_of(rank * block, block), block), :]
            used = at < total
            starts = [pl.multiple_of(tile_ref[c, at] * 128, 128) for c in range(foot)]
            for c, start in enumerate(starts):
                taper = tapers[owner, pl.ds(rank * foot + c, 1), :]
                part = jnp.dot(
                    weight, model_ref[:, pl.ds(start, 128)], preferred_element_type=jnp.float32
                )
                scaled = part * taper
                results.append((start, jnp.where(used, scaled, 0.0)))
        for start, scaled in results:
            out_ref[:, pl.ds(start, 128)] += scaled
        return carry

    lax.fori_loop(0, (total + GROUP - 1) // GROUP, turn, 0)


def body(
    members, predicted, perturbation, observed, noise_std, taper_weights, foot_brick, foot_tiles
):
    mem_count = lax.axis_size("mem")
    brick_count = lax.axis_size("brick")
    part, gates, wide = predicted.shape
    ensemble = part * brick_count
    local = wide // brick_count
    block = ensemble // mem_count
    foot = foot_tiles.shape[1]
    foot_length = taper_weights.shape[1]
    devices = mem_count * brick_count
    cap = max(2, 2 * local // brick_count)
    slots = devices * cap
    vmem = pltpu.CompilerParams(vmem_limit_bytes=24 * 1024 * 1024)
    in_vmem = pl.BlockSpec(memory_space=pltpu.VMEM)
    in_smem = pl.BlockSpec(memory_space=pltpu.SMEM)

    model_all = lax.all_gather(members.astype(jnp.bfloat16), "mem", axis=0, tiled=True)

    pair = jnp.concatenate([predicted, perturbation], axis=1).astype(jnp.bfloat16)
    pair = jnp.transpose(pair, (2, 0, 1))
    pair = jnp.pad(pair, ((0, 0), (0, 0), (0, 128 - 2 * gates)))
    pair = pair.reshape(brick_count, local, part, 128)
    destination = foot_brick[:, 0]
    order = jnp.arange(local)
    before = order[None, :] < order[:, None]
    rank = jnp.sum(
        ((destination[:, None] == destination[None, :]) & before).astype(jnp.int32), axis=1
    )
    slot_of = destination * cap + rank
    hot = slot_of[None, :] == jnp.arange(brick_count * cap, dtype=jnp.int32)[:, None]
    index = jnp.sum(jnp.where(hot, order[None, :], 0), axis=1)
    numbers = jnp.concatenate([foot_tiles, jnp.ones((local, 1), jnp.int32)], axis=1)
    numbers = jnp.pad(numbers.astype(jnp.bfloat16), ((0, 0), (0, 127 - foot)))
    extra = jnp.concatenate([taper_weights, numbers], axis=1)
    extra = jnp.dot(hot.astype(jnp.bfloat16), extra, preferred_element_type=jnp.float32)
    extra = extra.astype(jnp.bfloat16)
    taper_slots = extra[:, :foot_length].reshape(brick_count, cap * foot, 128)
    number_slots = extra[:, foot_length:].reshape(brick_count, cap, 128)
    tail = -(-cap * (foot + 1) // 16) * 16
    taper_slots = jnp.concatenate([taper_slots, number_slots], axis=1)
    taper_slots = jnp.pad(taper_slots, ((0, 0), (0, tail - cap * (foot + 1)), (0, 0)))

    out_rows = cap * block + tail
    recv = pl.pallas_call(
        owner_kernel,
        out_shape=jax.ShapeDtypeStruct((mem_count, brick_count, out_rows, 128), jnp.bfloat16),
        in_specs=[in_smem] + [in_vmem] * 4,
        out_specs=in_vmem,
        scratch_shapes=[
            pltpu.VMEM(pair.shape, jnp.bfloat16),
            pltpu.VMEM((local, gates, ensemble), jnp.float32),
            pltpu.VMEM((local, gates, ensemble), jnp.float32),
            pltpu.VMEM((local, gates, gates), jnp.float32),
            pltpu.VMEM((gates, gates, local), jnp.float32),
            pltpu.VMEM((local, gates, gates), jnp.float32),
            pltpu.VMEM((brick_count, cap * gates + tail, 128), jnp.bfloat16),
            pltpu.VMEM((brick_count, cap * gates, 128), jnp.bfloat16),
            pltpu.VMEM((brick_count, cap * gates + tail, 128), jnp.bfloat16),
            pltpu.VMEM((brick_count, cap * gates, 128), jnp.bfloat16),
            pltpu.VMEM((brick_count, mem_count, out_rows, 128), jnp.bfloat16),
        ]
        + [pltpu.SemaphoreType.DMA((brick_count * PIECES,))] * 2
        + [pltpu.SemaphoreType.DMA((brick_count,))] * 4
        + [pltpu.SemaphoreType.DMA((brick_count * mem_count,))] * 2,
        compiler_params=pltpu.CompilerParams(
            vmem_limit_bytes=24 * 1024 * 1024, collective_id=0, has_side_effects=True
        ),
        cost_estimate=pl.CostEstimate(
            flops=20_000_000_000, bytes_accessed=200_000_000, transcendentals=0
        ),
    )(
        index,
        pair,
        jnp.transpose(observed)[:, :, None],
        jnp.transpose(noise_std)[:, :, None],
        taper_slots,
    ).reshape(devices, out_rows, 128)

    numbers = recv[:, cap * (block + foot) : cap * (block + foot + 1), : foot + 1]
    numbers = numbers.astype(jnp.float32).astype(jnp.int32).reshape(slots, foot + 1)
    filled = numbers[:, foot] == 1
    spots = jnp.arange(slots)
    position = jnp.sum((filled[None, :] & (spots[None, :] < spots[:, None])).astype(jnp.int32), axis=1)
    listed = filled[None, :] & (position[None, :] == spots[:, None])
    slot_list = jnp.sum(jnp.where(listed, spots[None, :], 0), axis=1)
    tile_list = jnp.sum(
        jnp.where(listed[None], jnp.transpose(numbers[:, :foot])[:, None, :], 0), axis=2
    )
    count = jnp.sum(filled.astype(jnp.int32)).reshape(1)

    return pl.pallas_call(
        update_kernel,
        out_shape=jax.ShapeDtypeStruct(members.shape, members.dtype),
        in_specs=[in_smem] * 3 + [in_vmem] * 3,
        out_specs=in_vmem,
        scratch_shapes=[pltpu.VMEM((devices, cap * foot, 128), jnp.float32)],
        compiler_params=vmem,
        cost_estimate=pl.CostEstimate(flops=600_000_000, bytes_accessed=10_000_000, transcendentals=0),
    )(count, slot_list, tile_list, recv, model_all, members)


def solution(mesh):
    in_specs = (
        P("mem", "brick"),
        P("brick", None, "mem"),
        P("brick", None, "mem"),
        P(None, ("mem", "brick")),
        P(None, ("mem", "brick")),
        P(("mem", "brick"), None),
        P(("mem", "brick"), None),
        P(("mem", "brick"), None),
    )
    out_specs = P("mem", "brick")
    return jax.shard_map(body, mesh=mesh, in_specs=in_specs, out_specs=out_specs, check_vma=False)
```
